32 devices in a mesh: dp: 4 (over y, x), noise: 8 (over z, core).
Axes of the slice: x: 2, y: 2, z: 4, core: 2. Of those that a mesh axis runs over, the one named last changes fastest.
Arguments:
- prefix_rows: bfloat16 [2, 32, 816, 640], P(None, ('dp', 'noise')), may hold values from -6 to 6
- action_rows: bfloat16 [2, 32, 50, 1024], P(None, ('dp', 'noise')), may hold values from -6 to 6
- segment_item: int32 [2, 32], P(None, ('dp', 'noise')), may hold values from 0 to 7
- segment_time: int32 [2, 32], P(None, ('dp', 'noise')), may hold values from 0 to 15
- item_weight: int32 [2, 32], P(None, 'dp'), may hold values from 0 to 15
- prefix_len: int32 [2, 32], P(None, 'dp'), may hold values from 204 to 816, as said below
- vlm_prenorm: bfloat16 [640], P(('dp', 'noise')), may hold values from 0.5 to 1.5
- vlm_query: bfloat16 [640, 1024], P(('dp', 'noise')), may hold values from -0.25 to 0.25
- vlm_key: bfloat16 [640, 256], P(('dp', 'noise')), may hold values from -0.25 to 0.25
- vlm_value: bfloat16 [640, 256], P(('dp', 'noise')), may hold values from -0.25 to 0.25
- vlm_mixer: bfloat16 [1024, 640], P(('dp', 'noise')), may hold values from -1.5 to 1.5
- vlm_midnorm: bfloat16 [640], P(('dp', 'noise')), may hold values from 0.5 to 1.5
- vlm_gate: bfloat16 [640, 2048], P(('dp', 'noise')), may hold values from -0.25 to 0.25
- vlm_expand: bfloat16 [640, 2048], P(('dp', 'noise')), may hold values from -0.25 to 0.25
- vlm_down: bfloat16 [2048, 640], P(('dp', 'noise')), may hold values from -0.125 to 0.125
- act_prenorm: bfloat16 [1024], P(('dp', 'noise')), may hold values from 0.5 to 1.5
- act_query: bfloat16 [1024, 1024], P(('dp', 'noise')), may hold values from -0.1875 to 0.1875
- act_key: bfloat16 [1024, 256], P(('dp', 'noise')), may hold values from -0.1875 to 0.1875
- act_value: bfloat16 [1024, 256], P(('dp', 'noise')), may hold values from -0.1875 to 0.1875
- act_mixer: bfloat16 [1024, 1024], P(('dp', 'noise')), may hold values from -1.5 to 1.5
- act_midnorm: bfloat16 [1024], P(('dp', 'noise')), may hold values from 0.5 to 1.5
- act_gate: bfloat16 [1024, 4096], P(('dp', 'noise')), may hold values from -0.1875 to 0.1875
- act_expand: bfloat16 [1024, 4096], P(('dp', 'noise')), may hold values from -0.1875 to 0.1875
- act_down: bfloat16 [4096, 1024], P(('dp', 'noise')), may hold values from -0.09375 to 0.09375
- time_scales: bfloat16 [2048, 16], P(('dp', 'noise')), may hold values from 0.099609375 to 1.8984375
- cot_prefix: bfloat16 [2, 32, 816, 640], P(None, ('dp', 'noise')), may hold values from -6 to 6
- cot_action: bfloat16 [2, 32, 50, 1024], P(None, ('dp', 'noise')), may hold values from -6 to 6
Outputs:
- prefix_out: bfloat16 [2, 32, 816, 640], P(None, ('dp', 'noise'))
- action_out: bfloat16 [2, 32, 50, 1024], P(None, ('dp', 'noise'))
- prefix_grad: float32 [2, 32, 816, 640], P(None, ('dp', 'noise'))
- action_grad: float32 [2, 32, 50, 1024], P(None, ('dp', 'noise'))
- prefgrad_prenorm: float32 [640], P(('dp', 'noise'))
- prefgrad_query: float32 [640, 1024], P(('dp', 'noise'))
- prefgrad_key: float32 [640, 256], P(('dp', 'noise'))
- prefgrad_value: float32 [640, 256], P(('dp', 'noise'))
- prefgrad_mixer: float32 [1024, 640], P(('dp', 'noise'))
- prefgrad_midnorm: float32 [640], P(('dp', 'noise'))
- prefgrad_gate: float32 [640, 2048], P(('dp', 'noise'))
- prefgrad_expand: float32 [640, 2048], P(('dp', 'noise'))
- prefgrad_down: float32 [2048, 640], P(('dp', 'noise'))
- actgrad_prenorm: float32 [1024], P(('dp', 'noise'))
- actgrad_query: float32 [1024, 1024], P(('dp', 'noise'))
- actgrad_key: float32 [1024, 256], P(('dp', 'noise'))
- actgrad_value: float32 [1024, 256], P(('dp', 'noise'))
- actgrad_mixer: float32 [1024, 1024], P(('dp', 'noise'))
- actgrad_midnorm: float32 [1024], P(('dp', 'noise'))
- actgrad_gate: float32 [1024, 4096], P(('dp', 'noise'))
- actgrad_expand: float32 [1024, 4096], P(('dp', 'noise'))
- actgrad_down: float32 [4096, 1024], P(('dp', 'noise'))
- scales_grad: float32 [2048, 16], P(('dp', 'noise'))
The draws below stay inside these ranges and needn't reach their ends.
Inputs may be any that keep to these rules, and one draw needn't show every extreme that they name: `segment_item`: numbers the segment's item within its data group of 8 items. `prefix_len`: prefix keys at positions of len or later are never attended.
All inputs are finite; a program needn't handle non-finite values.
Results may differ from the reference program's by a relative error of at most 0.015.
Values may be sent and summed in bfloat16 or wider, within the bound.
No kernel may reach another device: no remote copies, remote signals or barrier semaphores. Data moves between devices by JAX's collectives and lax.ppermute only.
A program may use at most 448 MiB of HBM per device.

```python
import math
import jax
import jax.numpy as jnp
import numpy as np
from jax import lax

D = 640
HEAD_DIM = 256
FF = 2048
A = 1024
FFA = 4096
PREFIX = 816
SEG_LEN = 50
TIMES = 16
MICRO = 2
SEG_DEV = 1
HQ = 1024
GROUP = 8
GROUP_SEGS = 8
ITEMS = 32
SEGMENTS = 32


def draw_prefix_len(key, part):
    first, second = jax.random.split(key)
    base = jax.random.randint(first, (MICRO, ITEMS), PREFIX // 4, PREFIX + 1)
    picked = jax.random.randint(second, (MICRO, 1), 0, ITEMS)
    column = jnp.arange(ITEMS)[None, :]
    shorter = jnp.where(column == (picked + 1) % ITEMS, PREFIX // 4, base)
    return jnp.where(column == picked, PREFIX, shorter).astype(jnp.int32)


def place_ends(result, own_key, smallest, top_value):
    dims = result.shape
    place = [jax.random.randint(jax.random.fold_in(own_key, axis), (), 0, dims[axis]) for axis in range(len(dims))]
    result = result.at[tuple(place)].set(smallest)
    longest = dims.index(max(dims))
    place[longest] = (place[longest] + 1) % dims[longest]
    return result.at[tuple(place)].set(top_value)


def with_spikes(values, key, source, target, shards_of, factor):
    owner, partner = [(jnp.arange(values.shape[position]) // (values.shape[position] // shards_of)).reshape([-1 if axis == position else 1 for axis in range(values.ndim)]) for position in (source, target)]
    chosen = jax.random.permutation(key, shards_of)[partner]
    strong = (owner == chosen) | (owner == (partner + shards_of // 2) % shards_of)
    return jnp.where(strong, factor * values, values)


def steps_of(key, shape, shards, least, high):
    loudness, own = 1.0, jax.random.fold_in(key, 6)
    for axis_at, blocks in shards:
        draws = jnp.exp(jax.random.uniform(jax.random.fold_in(own, axis_at), (blocks,), jnp.float32, least / len(shards), high / len(shards)))
        loudness = loudness * jnp.repeat(draws, shape[axis_at] // blocks).reshape([-1 if axis == axis_at else 1 for axis in range(len(shape))])
    return loudness


def rank_table(count, slope):
    portions = [(1 << 20) // math.isqrt(grade ** slope) + 1 for grade in range(1, count + 1)]
    scale = 1 + sum(portions) // (1 << 30)
    return np.cumsum(np.array([max(1, weight // scale) for weight in portions]))


def skewed_ids(rng, shape, amount, lean):
    listing = rank_table(amount, lean)
    ticket = jax.random.randint(jax.random.fold_in(rng, 1), shape, 0, int(listing[amount - 1]))
    standing = jnp.searchsorted(jnp.asarray(listing, jnp.int32), ticket, side="right")
    return jax.random.permutation(jax.random.fold_in(rng, 2), amount)[standing].astype(jnp.int32)


def noise(stream_key, dims, scale, bound, pieces=(), kind=jnp.bfloat16):
    entries = scale * jax.random.normal(stream_key, dims, jnp.float32)
    if pieces:
        entries = entries * steps_of(stream_key, dims, pieces, -0.22, 0.18)
    return jnp.clip(entries, -bound, bound).astype(kind)


def bell_draw_with(rng, extent, spread, bound, cuts, heavy, held_as=jnp.bfloat16):
    result = spread * jax.random.normal(rng, extent, jnp.float32)
    if cuts:
        result = result * steps_of(rng, extent, cuts, -0.22, 0.18)
    return jnp.clip(with_spikes(result, jax.random.fold_in(rng, 3), *heavy), -bound, bound).astype(held_as)


def setup_inputs(seed: int = 0) -> dict:
    key_list = jax.random.split(jax.random.key(seed), 28)
    prefix_rows = noise(key_list[0], (MICRO, ITEMS, PREFIX, D), 1.0, 6.0, ((1, 32),))
    action_rows = noise(key_list[1], (MICRO, SEGMENTS, SEG_LEN, A), 1.0, 6.0, ((1, 32),))
    segment_item = place_ends(skewed_ids(key_list[2], (MICRO, SEGMENTS), GROUP, 2), jax.random.fold_in(key_list[2], 3), 0, GROUP - 1).astype(jnp.int32)
    segment_time = place_ends(jax.random.randint(key_list[3], (MICRO, SEGMENTS), 0, TIMES), jax.random.fold_in(key_list[3], 1), 0, TIMES - 1).astype(jnp.int32)
    item_weight = place_ends(skewed_ids(key_list[4], (MICRO, ITEMS), 16, 2), jax.random.fold_in(key_list[4], 3), 0, 15).astype(jnp.int32)
    prefix_len = draw_prefix_len(jax.random.fold_in(key_list[27], 71), 0)
    vlm_prenorm = jnp.clip(1.0 + 0.1 * jax.random.normal(key_list[6], (D,), jnp.float32), 0.5, 1.5).astype(jnp.bfloat16)
    vlm_query = noise(key_list[7], (D, HQ), D ** -0.5, 0.25, ((0, 32),))
    vlm_key = noise(key_list[8], (D, HEAD_DIM), D ** -0.5, 0.25, ((0, 32),))
    vlm_value = noise(key_list[9], (D, HEAD_DIM), D ** -0.5, 0.25, ((0, 32),))
    vlm_mixer = noise(key_list[10], (HQ, D), (max(HQ // 64, 1)) ** -0.5, 1.5, ((0, 32),))
    vlm_midnorm = jnp.clip(1.0 + 0.1 * jax.random.normal(key_list[11], (D,), jnp.float32), 0.5, 1.5).astype(jnp.bfloat16)
    vlm_gate = noise(key_list[12], (D, FF), D ** -0.5, 0.25, ((0, 32),))
    vlm_expand = noise(key_list[13], (D, FF), D ** -0.5, 0.25, ((0, 32),))
    vlm_down = noise(key_list[14], (FF, D), FF ** -0.5, 0.125, ((0, 32),))
    act_prenorm = jnp.clip(1.0 + 0.1 * jax.random.normal(key_list[15], (A,), jnp.float32), 0.5, 1.5).astype(jnp.bfloat16)
    act_query = noise(key_list[16], (A, HQ), A ** -0.5, 0.1875, ((0, 32),))
    act_key = noise(key_list[17], (A, HEAD_DIM), A ** -0.5, 0.1875, ((0, 32),))
    act_value = noise(key_list[18], (A, HEAD_DIM), A ** -0.5, 0.1875, ((0, 32),))
    act_mixer = noise(key_list[19], (HQ, A), (max(HQ // 64, 1)) ** -0.5, 1.5, ((0, 32),))
    act_midnorm = jnp.clip(1.0 + 0.1 * jax.random.normal(key_list[20], (A,), jnp.float32), 0.5, 1.5).astype(jnp.bfloat16)
    act_gate = noise(key_list[21], (A, FFA), A ** -0.5, 0.1875, ((0, 32),))
    act_expand = noise(key_list[22], (A, FFA), A ** -0.5, 0.1875, ((0, 32),))
    act_down = noise(key_list[23], (FFA, A), FFA ** -0.5, 0.09375, ((0, 32),))
    time_scales = jnp.clip(1.0 + 0.18 * jax.random.normal(key_list[24], (2 * A, TIMES), jnp.float32), 0.099609375, 1.8984375).astype(jnp.bfloat16)
    cot_prefix = bell_draw_with(key_list[25], (MICRO, ITEMS, PREFIX, D), 1.0, 6.0, ((1, 32),), (1, 3, 32, 2.75))
    cot_action = bell_draw_with(key_list[26], (MICRO, SEGMENTS, SEG_LEN, A), 1.0, 6.0, ((1, 32),), (1, 3, 32, 2.75))
    return {"prefix_rows": prefix_rows, "action_rows": action_rows, "segment_item": segment_item, "segment_time": segment_time, "item_weight": item_weight, "prefix_len": prefix_len, "vlm_prenorm": vlm_prenorm, "vlm_query": vlm_query, "vlm_key": vlm_key, "vlm_value": vlm_value, "vlm_mixer": vlm_mixer, "vlm_midnorm": vlm_midnorm, "vlm_gate": vlm_gate, "vlm_expand": vlm_expand, "vlm_down": vlm_down, "act_prenorm": act_prenorm, "act_query": act_query, "act_key": act_key, "act_value": act_value, "act_mixer": act_mixer, "act_midnorm": act_midnorm, "act_gate": act_gate, "act_expand": act_expand, "act_down": act_down, "time_scales": time_scales, "cot_prefix": cot_prefix, "cot_action": cot_action}


EPS = 1e-06
HIGH = lax.Precision.HIGHEST

@jax.custom_vjp
def low(v):
    return lax.optimization_barrier(v.astype(jnp.bfloat16)).astype(jnp.float32)

@jax.custom_vjp
def low_back(v):
    return v

def low_keep(v):
    return (low(v), None)

def low_pass(kept, grad):
    return (grad,)

def back_keep(v):
    return (v, None)

def back_low(kept, grad):
    return (low(grad),)
low.defvjp(low_keep, low_pass)
low_back.defvjp(back_keep, back_low)

def matmul(left, right):
    return jnp.dot(left, right, precision=HIGH)

def normed(rows):
    return rows * lax.rsqrt(lax.optimization_barrier(jnp.mean(rows * rows, axis=-1, keepdims=True)) + EPS)

def attention(queries, keys, values, valid):
    batch, rows, width = queries.shape
    depth = keys.shape[-1]
    split = queries.reshape(batch, rows, width // depth, depth)
    raw = jnp.einsum('bnhd,bmd->bhnm', split, keys, precision=HIGH)
    scores = low_back(raw) * depth ** (-0.5)
    scores = jnp.where(valid[:, None, None, :], scores, -1e+30)
    top = lax.optimization_barrier(jnp.max(scores, axis=-1, keepdims=True))
    expo = jnp.exp(scores - top)
    probs = expo / lax.optimization_barrier(jnp.sum(expo, axis=-1, keepdims=True))
    mixed = jnp.einsum('bhnm,bmd->bnhd', low(probs), values, precision=HIGH)
    return low_back(low(mixed.reshape(batch, rows, width)))

def feed(hidden, w_gate, w_up, w_down):
    gate = low_back(matmul(hidden, w_gate))
    upward = low_back(matmul(hidden, w_up))
    middle = low(jax.nn.gelu(gate) * upward)
    return low_back(matmul(middle, w_down))

def reference(prefix_rows, action_rows, segment_item, segment_time, item_weight, prefix_len, vlm_prenorm, vlm_query, vlm_key, vlm_value, vlm_mixer, vlm_midnorm, vlm_gate, vlm_expand, vlm_down, act_prenorm, act_query, act_key, act_value, act_mixer, act_midnorm, act_gate, act_expand, act_down, time_scales, cot_prefix, cot_action):
    params = tuple((weight.astype(jnp.float32) for weight in (vlm_prenorm, vlm_query, vlm_key, vlm_value, vlm_mixer, vlm_midnorm, vlm_gate, vlm_expand, vlm_down, act_prenorm, act_query, act_key, act_value, act_mixer, act_midnorm, act_gate, act_expand, act_down, time_scales)))
    positions = jnp.arange(PREFIX).astype(jnp.int32)
    blocks = SEGMENTS // SEG_DEV
    prefix_outs = []
    action_outs = []
    prefix_grads = []
    action_grads = []
    totals = None
    for step in range(MICRO):
        owner = (jnp.arange(SEGMENTS) // GROUP_SEGS * GROUP + segment_item[step]).astype(jnp.int32)
        seg_len = prefix_len[step][owner]
        seg_weight = (item_weight[step][owner] + 1).astype(jnp.float32) / 8.0
        times = segment_time[step]
        lens = prefix_len[step]

        def forward(weights, prefix_in, action_in):
            pre_gain, pre_query, pre_key, pre_value, pre_mixer, pre_midgain, pre_gate, pre_expand, pre_down, suf_gain, suf_query, suf_key, suf_value, suf_mixer, suf_midgain, suf_gate, suf_expand, suf_down, time_table = weights

            def item_kv(rows):
                hidden = low(normed(rows) * pre_gain)
                return (matmul(hidden, pre_key), matmul(hidden, pre_value))
            keys_raw, values_raw = lax.map(jax.checkpoint(item_kv), prefix_in)
            all_keys = low_back(low(keys_raw))
            all_values = low_back(low(values_raw))

            def prefix_item(args):
                rows, keys, values, length = args
                hidden = low(normed(rows) * pre_gain)
                queries = low_back(low(matmul(hidden, pre_query)))
                valid = positions < length
                mixed = attention(queries[None], keys[None], values[None], valid[None])[0]
                resid = rows + low_back(matmul(mixed, pre_mixer))
                return resid + feed(low(normed(resid) * pre_midgain), pre_gate, pre_expand, pre_down)
            prefix_out = lax.map(jax.checkpoint(prefix_item), (prefix_in, all_keys, all_values, lens))

            def action_block(args):
                rows, owners, levels, lengths = args
                hot = (levels[:, None] == jnp.arange(TIMES)[None, :]).astype(rows.dtype)
                mods = jnp.dot(hot, time_table.T, precision=HIGH)
                first_mod = mods[:, None, :A]
                second_mod = mods[:, None, A:]
                hidden = low(normed(rows) * suf_gain * first_mod)
                queries = low_back(low(matmul(hidden, suf_query)))
                own_keys = low_back(low(matmul(hidden, suf_key)))
                own_values = low_back(low(matmul(hidden, suf_value)))
                keys = jnp.concatenate([all_keys[owners], own_keys], axis=1)
                values = jnp.concatenate([all_values[owners], own_values], axis=1)
                valid = jnp.concatenate([positions[None, :] < lengths[:, None], jnp.ones((rows.shape[0], SEG_LEN), dtype=bool)], axis=1)
                mixed = attention(queries, keys, values, valid)
                resid = rows + low_back(matmul(mixed, suf_mixer))
                return resid + feed(low(normed(resid) * suf_midgain * second_mod), suf_gate, suf_expand, suf_down)
            action_out = lax.map(jax.checkpoint(action_block), (action_in.reshape(blocks, SEG_DEV, SEG_LEN, A), owner.reshape(blocks, SEG_DEV), times.reshape(blocks, SEG_DEV), seg_len.reshape(blocks, SEG_DEV)))
            return (prefix_out, action_out.reshape(SEGMENTS, SEG_LEN, A))
        outputs, pullback = jax.vjp(forward, params, prefix_rows[step].astype(jnp.float32), action_rows[step].astype(jnp.float32))
        grad_params, grad_prefix, grad_action = pullback((cot_prefix[step].astype(jnp.float32), cot_action[step].astype(jnp.float32) * seg_weight[:, None, None]))
        prefix_outs.append(outputs[0].astype(jnp.bfloat16))
        action_outs.append(outputs[1].astype(jnp.bfloat16))
        prefix_grads.append(grad_prefix)
        action_grads.append(grad_action)
        totals = grad_params if totals is None else tuple((left + right for left, right in zip(totals, grad_params)))
    return (jnp.stack(prefix_outs), jnp.stack(action_outs), jnp.stack(prefix_grads), jnp.stack(action_grads), totals[0], totals[1], totals[2], totals[3], totals[4], totals[5], totals[6], totals[7], totals[8], totals[9], totals[10], totals[11], totals[12], totals[13], totals[14], totals[15], totals[16], totals[17], totals[18])
```

```python
import jax
import jax.numpy as jnp
from jax import lax
from jax.sharding import PartitionSpec as P

EPS = 1e-06
HIGH = lax.Precision.HIGHEST


def normed(rows):
    factor = lax.rsqrt(jnp.mean(rows * rows, axis=-1, keepdims=True) + EPS)
    return (rows * factor, factor)


def norm_back(grad_hidden, normal, factor, gain_mod):
    grad_normal = grad_hidden * gain_mod
    centred = jnp.mean(grad_normal * normal, axis=-1, keepdims=True)
    return factor * (grad_normal - normal * centred)


def flatten(array):
    return array.reshape(-1, array.shape[-1])


def weight_grad(inputs, grads):
    return jnp.einsum(
        "ra,rb->ab", flatten(inputs), flatten(grads), preferred_element_type=jnp.float32
    )


def back_through(grads, weight):
    return jnp.einsum("...b,ab->...a", grads, weight, preferred_element_type=jnp.float32)


def scores_of(queries, keys, valid):
    batch, rows, width = queries.shape
    depth = keys.shape[-1]
    split = queries.reshape(batch, rows, width // depth, depth)
    scores = jnp.einsum(
        "bnhd,bmd->bhnm", split, keys, preferred_element_type=jnp.float32
    ) * depth ** (-0.5)
    return (split, jnp.where(valid[:, None, None, :], scores, -1e30))


def attend(queries, keys, values, valid):
    split, scores = scores_of(queries, keys, valid)
    top = jnp.max(scores, axis=-1, keepdims=True)
    total = top + jnp.log(jnp.sum(jnp.exp(scores - top), axis=-1, keepdims=True))
    probs = jnp.exp(scores - total).astype(jnp.bfloat16)
    mixed = jnp.einsum("bhnm,bmd->bnhd", probs, values, preferred_element_type=jnp.float32)
    return (mixed.reshape(queries.shape).astype(jnp.bfloat16), total)


def attend_back(queries, keys, values, valid, total, grad_mixed):
    split, scores = scores_of(queries, keys, valid)
    depth = keys.shape[-1]
    probs = jnp.exp(scores - total)
    grad_split = grad_mixed.reshape(split.shape)
    grad_values = jnp.einsum(
        "bhnm,bnhd->bmd", probs.astype(jnp.bfloat16), grad_split, preferred_element_type=jnp.float32
    )
    grad_probs = jnp.einsum(
        "bnhd,bmd->bhnm", grad_split, values, preferred_element_type=jnp.float32
    )
    centred = jnp.sum(probs * grad_probs, axis=-1, keepdims=True)
    grad_scores = (probs * (grad_probs - centred) * depth ** (-0.5)).astype(jnp.bfloat16)
    grad_queries = jnp.einsum(
        "bhnm,bmd->bnhd", grad_scores, keys, preferred_element_type=jnp.float32
    )
    grad_keys = jnp.einsum("bhnm,bnhd->bmd", grad_scores, split, preferred_element_type=jnp.float32)
    return (grad_queries.reshape(queries.shape).astype(jnp.bfloat16), grad_keys, grad_values)


ALL = ("dp", "noise")


def gelu_parts(gate):
    c = 0.7978845608028654
    inner = c * (gate + 0.044715 * gate * gate * gate)
    t = jnp.tanh(inner)
    half = 0.5 * (1.0 + t)
    slope = half + 0.5 * gate * (1.0 - t * t) * c * (1.0 + 3 * 0.044715 * gate * gate)
    return gate * half, slope


def swap_bit(x, bit, total):
    return lax.ppermute(x, ALL, [(i, i ^ (1 << bit)) for i in range(total)])


def scatter_sum(x, order, total):
    me = lax.axis_index("dp") * lax.axis_size("noise") + lax.axis_index("noise")
    live = list(range(total.bit_length() - 2, -1, -1))
    rest = x.shape[1:]
    for bit in order:
        at = live.index(bit)
        high, low = 1 << at, 1 << (len(live) - at - 1)
        x = x.reshape((high, 2, low) + rest)
        mine = (me >> bit) & 1
        keep = lax.dynamic_index_in_dim(x, mine, 1, keepdims=False)
        send = lax.dynamic_index_in_dim(x, 1 - mine, 1, keepdims=False)
        x = keep + swap_bit(send, bit, total)
        live.remove(bit)
    return x.reshape(rest)


def orders(total):
    bits = list(range(1, total.bit_length() - 1))
    high = bits[::-1]
    third = len(bits) // 2
    return ([0] + high, [0] + high[1:] + high[:1], [0] + bits)


def own_attend(q, k, v, keys, values, valid):
    depth = keys.shape[-1]
    scale = depth ** (-0.5)
    far = jnp.einsum("nmqhd,mkd->mhnqk", q, keys, preferred_element_type=jnp.float32) * scale
    far = jnp.where(valid[:, None, None, None, :], far, -1e30)
    near = jnp.einsum("nmqhd,nmkd->mhnqk", q, k, preferred_element_type=jnp.float32) * scale
    top = jnp.maximum(jnp.max(far, -1, keepdims=True), jnp.max(near, -1, keepdims=True))
    efar, enear = jnp.exp(far - top), jnp.exp(near - top)
    total = jnp.sum(efar, -1, keepdims=True) + jnp.sum(enear, -1, keepdims=True)
    pfar, pnear = efar / total, enear / total
    mixed = jnp.einsum("mhnqk,mkd->nmqhd", pfar.astype(jnp.bfloat16), values, preferred_element_type=jnp.float32)
    mixed = mixed + jnp.einsum("mhnqk,nmkd->nmqhd", pnear.astype(jnp.bfloat16), v, preferred_element_type=jnp.float32)
    return mixed, pfar, pnear


def own_attend_back(q, k, v, keys, values, pfar, pnear, dout):
    depth = keys.shape[-1]
    scale = depth ** (-0.5)
    dvalues = jnp.einsum("mhnqk,nmqhd->mkd", pfar.astype(jnp.bfloat16), dout, preferred_element_type=jnp.float32)
    dv = jnp.einsum("mhnqk,nmqhd->nmkd", pnear.astype(jnp.bfloat16), dout, preferred_element_type=jnp.float32)
    dfar = jnp.einsum("nmqhd,mkd->mhnqk", dout, values, preferred_element_type=jnp.float32)
    dnear = jnp.einsum("nmqhd,nmkd->mhnqk", dout, v, preferred_element_type=jnp.float32)
    centre = jnp.sum(pfar * dfar, -1, keepdims=True) + jnp.sum(pnear * dnear, -1, keepdims=True)
    sfar = (pfar * (dfar - centre) * scale).astype(jnp.bfloat16)
    snear = (pnear * (dnear - centre) * scale).astype(jnp.bfloat16)
    dq = jnp.einsum("mhnqk,mkd->nmqhd", sfar, keys, preferred_element_type=jnp.float32)
    dq = dq + jnp.einsum("mhnqk,nmkd->nmqhd", snear, k, preferred_element_type=jnp.float32)
    dkeys = jnp.einsum("mhnqk,nmqhd->mkd", sfar, q, preferred_element_type=jnp.float32)
    dk = jnp.einsum("mhnqk,nmqhd->nmkd", snear, q, preferred_element_type=jnp.float32)
    return dq, dk, dv, dkeys, dvalues


def dot(a, b):
    return jnp.dot(a, b, preferred_element_type=jnp.float32)


def dot_t(a, b):
    return lax.dot_general(a, b, (((1,), (1,)), ((), ())), preferred_element_type=jnp.float32)


def dot_w(a, b):
    return lax.dot_general(a, b, (((0,), (0,)), ((), ())), preferred_element_type=jnp.float32)


def per_device(
    prefix_rows,
    action_rows,
    segment_item,
    segment_time,
    item_weight,
    prefix_len,
    vlm_prenorm,
    vlm_query,
    vlm_key,
    vlm_value,
    vlm_mixer,
    vlm_midnorm,
    vlm_gate,
    vlm_expand,
    vlm_down,
    act_prenorm,
    act_query,
    act_key,
    act_value,
    act_mixer,
    act_midnorm,
    act_gate,
    act_expand,
    act_down,
    time_scales,
    cot_prefix,
    cot_action,
):
    bf = jnp.bfloat16
    micro, items, prefix, width = prefix_rows.shape
    seg_len, wide = action_rows.shape[2:]
    groups, n = lax.axis_size("dp"), lax.axis_size("noise")
    total = groups * n
    depth = vlm_key.shape[1]
    hq = vlm_query.shape[1]
    heads = hq // depth
    ff = vlm_gate.shape[1]
    ffa = act_gate.shape[1]
    levels = time_scales.shape[1]
    rows_p, rows_a = vlm_query.shape[0], act_query.shape[0]
    here = lax.axis_index("noise")
    live = micro * seg_len
    pad = -live % 16 if -live % 16 >= micro else -live % 16 + 16
    block = live + pad

    def padded(x):
        return jnp.pad(x.reshape(live, x.shape[-1]), ((0, pad), (0, 0)))

    extra = jnp.zeros((rows_p, 128), bf)
    extra = extra.at[:, 0].set(vlm_prenorm).at[:, 1].set(vlm_midnorm)
    pre_a = lax.all_gather(
        jnp.concatenate([vlm_query, vlm_key, vlm_value, extra], axis=1), ALL, axis=0, tiled=True
    )
    extra = jnp.concatenate(
        [
            act_prenorm[:, None],
            act_midnorm[:, None],
            time_scales.reshape(rows_a, -1),
            jnp.zeros((rows_a, 128 - 2 - time_scales.size // rows_a), bf),
        ],
        axis=1,
    )
    act_a = lax.all_gather(
        jnp.concatenate([act_query, act_key, act_value, act_mixer, extra], axis=1),
        ALL,
        axis=0,
        tiled=True,
    )
    pre_b = lax.all_gather(jnp.concatenate([vlm_gate, vlm_expand], axis=1), ALL, axis=0, tiled=True)
    pre_c = lax.all_gather(jnp.concatenate([vlm_mixer, vlm_down], axis=0), ALL, axis=0)
    unit = act_down.shape[0]
    cols = jnp.stack([act_gate, act_expand]).reshape(2, rows_a, groups, n, unit)
    cols = lax.all_to_all(
        cols.transpose(3, 0, 1, 2, 4).reshape(n, 2, rows_a, groups * unit), "noise", 0, 0, tiled=True
    )
    hidden_w = lax.all_gather(
        jnp.concatenate(
            [
                cols.transpose(0, 2, 1, 3).reshape(n * rows_a, 2 * groups * unit),
                act_down.reshape(-1, 2 * groups * unit),
            ],
            axis=0,
        ),
        "dp",
        axis=0,
    )
    part = groups * unit
    gu_w = hidden_w[:, : n * rows_a].reshape(groups * n * rows_a, 2 * part)
    down_w = hidden_w[:, n * rows_a :].reshape(part, wide)

    pre_qkv = pre_a[:, : hq + 2 * depth]
    pre_gain = pre_a[:, hq + 2 * depth].astype(jnp.float32)
    pre_midgain = pre_a[:, hq + 2 * depth + 1].astype(jnp.float32)
    pre_mixer = pre_c[:, : vlm_mixer.shape[0]].reshape(hq, width)
    pre_down = pre_c[:, vlm_mixer.shape[0] :].reshape(ff, width)
    suf_qkv = act_a[:, : hq + 2 * depth]
    suf_mixer = act_a[:, hq + 2 * depth : hq + 2 * depth + wide]
    small = act_a[:, hq + 2 * depth + wide :].astype(jnp.float32)
    suf_gain, suf_midgain = small[:, 0], small[:, 1]
    table = small[:, 2 : 2 + time_scales.size // rows_a].reshape(2 * wide, levels)

    item = segment_item[:, 0]
    time_hot = (segment_time[:, 0][:, None] == jnp.arange(levels)[None, :]).astype(jnp.float32)
    mods = jnp.einsum("mt,jt->mj", time_hot, table, precision=HIGH)
    mod1, mod2 = mods[:, None, :wide], mods[:, None, wide:]
    hot = item[:, None] == jnp.arange(prefix_len.shape[1])[None, :]
    weight = (jnp.sum(jnp.where(hot, item_weight, 0), axis=1) + 1).astype(jnp.float32) / 8.0
    grad_action = cot_action[:, 0].astype(jnp.float32) * weight[:, None, None]
    dy_own = padded(grad_action.astype(bf))
    dy_all = lax.all_gather(dy_own, "noise", axis=0, tiled=True)
    action_in = action_rows[:, 0].astype(jnp.float32)
    an1, as1 = normed(action_in)
    ah1 = padded((an1 * suf_gain * mod1).astype(bf))
    aqkv = dot(ah1, suf_qkv).astype(bf)
    tags = jnp.zeros((block, hq + 2 * depth), bf).at[live : live + micro, 0].set(item.astype(bf))
    gathered = lax.all_gather(aqkv + tags, "noise", axis=0)
    owned = gathered[:, live : live + micro, 0] == here.astype(bf)
    gathered = gathered[:, :live].reshape(n, micro, seg_len, hq + 2 * depth)
    qs = gathered[..., :hq].reshape(n, micro, seg_len, heads, depth)
    ks, vs = gathered[..., hq : hq + depth], gathered[..., hq + depth :]

    prefix_in = prefix_rows[:, 0].astype(jnp.float32)
    n1, s1 = normed(prefix_in)
    h1 = (n1 * pre_gain).astype(bf)
    qkv = jnp.einsum("mra,ab->mrb", h1, pre_qkv, preferred_element_type=jnp.float32).astype(bf)
    queries, keys, values = qkv[..., :hq], qkv[..., hq : hq + depth], qkv[..., hq + depth :]
    own_len = lax.dynamic_slice_in_dim(prefix_len, here, 1, axis=1)
    valid = jnp.arange(prefix, dtype=jnp.int32)[None, :] < own_len

    mixed, pfar, pnear = own_attend(qs, ks, vs, keys, values, valid)
    mixed = jnp.where(owned[:, :, None, None, None], mixed, 0.0).astype(bf).reshape(n, live, hq)
    mixed = jnp.pad(mixed, ((0, 0), (0, pad), (0, 0)))
    oa = lax.psum_scatter(mixed, "noise", scatter_dimension=0)
    a1 = action_in + dot(oa, suf_mixer)[:live].reshape(action_in.shape)
    an2, as2 = normed(a1)
    ah2 = padded((an2 * suf_midgain * mod2).astype(bf))
    h_all = lax.all_gather(ah2, "noise", axis=0, tiled=True)
    gu = dot(h_all, gu_w)
    gate_a, up_a = gu[:, :part], gu[:, part:]
    act_g, slope_g = gelu_parts(gate_a)
    mid_a = (act_g * up_a).astype(bf)
    out_part = dot(mid_a, down_w)
    dmid_a = dot_t(dy_all, down_w)
    dgu = jnp.concatenate(
        [(dmid_a * up_a * slope_g).astype(bf), (dmid_a * act_g).astype(bf)], axis=1
    )
    dh_part = dot_t(dgu, gu_w)
    both = jnp.concatenate([out_part, dh_part], axis=1).astype(bf).reshape(n, block, 2 * wide)
    both = lax.psum_scatter(both, "noise", scatter_dimension=0)[:live].astype(jnp.float32)
    action_out = (a1 + both[:, :wide].reshape(a1.shape)).astype(bf)
    grad_late = both[:, wide:].reshape(a1.shape)
    dgu_w = dot_w(h_all, dgu).astype(bf)
    ddown_w = dot_w(mid_a, dy_all).astype(bf)
    dff = lax.psum_scatter(
        jnp.concatenate(
            [
                dgu_w.reshape(groups, n * rows_a, 2 * part),
                ddown_w.reshape(groups, -1, 2 * part),
            ],
            axis=1,
        ),
        "dp",
        scatter_dimension=0,
    )
    ddown_a = dff[n * rows_a :].reshape(unit, wide)
    dgu_a = lax.all_to_all(
        dff[: n * rows_a].reshape(n, rows_a, 2 * part), "noise", 0, 0, tiled=True
    )
    dgu_a = dgu_a.reshape(n, rows_a, 2, groups, unit).transpose(2, 1, 3, 0, 4)
    dgu_a = dgu_a.reshape(2, rows_a, ffa)

    late_back = grad_late * an2
    suf_dmid = jnp.sum(late_back * mod2, axis=(0, 1))
    dmod2 = jnp.sum(late_back * suf_midgain, axis=1)
    da1 = grad_action + norm_back(grad_late, an2, as2, suf_midgain * mod2)
    dmixed_a = padded(da1.astype(bf))
    dattn_a = dot_t(dmixed_a, suf_mixer).astype(bf)
    dattn_all = lax.all_gather(dattn_a, "noise", axis=0)
    dattn_all = dattn_all[:, :live].reshape(n, micro, seg_len, hq)
    dattn_all = jnp.where(owned[:, :, None, None], dattn_all, 0).reshape(qs.shape)
    dqs, dks, dvs, far_dk, far_dv = own_attend_back(
        qs, ks, vs, keys, values, pfar, pnear, dattn_all
    )
    back = jnp.concatenate([dqs.reshape(n, live, hq), dks.reshape(n, live, depth), dvs.reshape(n, live, depth)], axis=-1)
    back = jnp.pad(back.astype(bf), ((0, 0), (0, pad), (0, 0)))
    daqkv = lax.psum_scatter(back, "noise", scatter_dimension=0)
    dah1 = dot_t(daqkv, suf_qkv)[:live].reshape(action_in.shape)
    first_back = dah1 * an1
    suf_dgain = jnp.sum(first_back * mod1, axis=(0, 1))
    dmod1 = jnp.sum(first_back * suf_gain, axis=1)
    action_grad = da1 + norm_back(dah1, an1, as1, suf_gain * mod1)
    dtable = jnp.einsum(
        "mj,mt->jt", jnp.concatenate([dmod1, dmod2], axis=-1), time_hot, precision=HIGH
    )
    dact_a = jnp.concatenate([dot_w(ah1, daqkv), dot_w(oa, dmixed_a)], axis=1).astype(bf)

    outs = [attend(queries[m : m + 1], keys[m : m + 1], values[m : m + 1], valid[m : m + 1]) for m in range(micro)]
    o = jnp.concatenate([x[0] for x in outs])
    x1 = prefix_in + jnp.einsum("mra,ab->mrb", o, pre_mixer, preferred_element_type=jnp.float32)
    n2, s2 = normed(x1)
    h2 = flatten((n2 * pre_midgain).astype(bf))
    gate = dot(h2, pre_b[:, :ff])
    up = dot(h2, pre_b[:, ff:])
    act, slope = gelu_parts(gate)
    mid = (act * up).astype(bf)
    prefix_out = (x1 + dot(mid, pre_down).reshape(x1.shape)).astype(bf)
    dy = flatten(cot_prefix[:, 0])
    dmid = dot_t(dy, pre_down)
    dgate = (dmid * up * slope).astype(bf)
    dup = (dmid * act).astype(bf)
    dh2 = (dot_t(dgate, pre_b[:, :ff]) + dot_t(dup, pre_b[:, ff:])).reshape(x1.shape)
    one, two, three = orders(total)
    ddown = scatter_sum(dot_w(mid, dy).astype(bf).reshape(total, -1, width), one, total)
    dgate_w = scatter_sum(dot_w(h2, dgate).astype(bf).reshape(total, rows_p, ff), two, total)
    dup_w = scatter_sum(dot_w(h2, dup).astype(bf).reshape(total, rows_p, ff), three, total)
    pre_dmid = jnp.sum(dh2 * n2, axis=(0, 1))
    dx1 = cot_prefix[:, 0].astype(jnp.float32) + norm_back(dh2, n2, s2, pre_midgain)
    dmixed = dx1.astype(bf)
    dattn = jnp.einsum("mrb,ab->mra", dmixed, pre_mixer, preferred_element_type=jnp.float32).astype(bf)
    dmixer = scatter_sum(dot_w(flatten(o), flatten(dmixed)).astype(bf).reshape(total, -1, width), one, total)
    dact_a = scatter_sum(dact_a.reshape(total, rows_a, -1), two, total)
    grads = [
        attend_back(queries[m : m + 1], keys[m : m + 1], values[m : m + 1], valid[m : m + 1], outs[m][1], dattn[m : m + 1])
        for m in range(micro)
    ]
    dk = jnp.concatenate([g[1] for g in grads]) + far_dk
    dv = jnp.concatenate([g[2] for g in grads]) + far_dv
    dqkv = jnp.concatenate([jnp.concatenate([g[0] for g in grads]), dk.astype(bf), dv.astype(bf)], axis=-1)
    dqkv_w = scatter_sum(dot_w(flatten(h1), flatten(dqkv)).astype(bf).reshape(total, rows_p, -1), three, total)
    dh1 = jnp.einsum("mrb,ab->mra", dqkv, pre_qkv, preferred_element_type=jnp.float32)
    pre_dgain = jnp.sum(dh1 * n1, axis=(0, 1))
    prefix_grad = dx1 + norm_back(dh1, n1, s1, pre_gain)
    smalls = jnp.concatenate(
        [
            dtable.reshape(total, -1),
            pre_dgain.reshape(total, rows_p),
            pre_dmid.reshape(total, rows_p),
            suf_dgain.reshape(total, rows_a),
            suf_dmid.reshape(total, rows_a),
        ],
        axis=1,
    )
    cut = smalls.shape[1]
    smalls = jnp.pad(smalls, ((0, 0), (0, -cut % 128))).reshape(total, -1, 128)
    smalls = scatter_sum(smalls, one, total).reshape(-1)
    f32 = jnp.float32
    at = dtable.size // total
    dact_a = dact_a.astype(f32)
    dqkv_w = dqkv_w.astype(f32)
    return (
        prefix_out[:, None],
        action_out[:, None],
        prefix_grad[:, None],
        action_grad[:, None],
        smalls[at : at + rows_p],
        dqkv_w[:, :hq],
        dqkv_w[:, hq : hq + depth],
        dqkv_w[:, hq + depth :],
        dmixer.astype(f32),
        smalls[at + rows_p : at + 2 * rows_p],
        dgate_w.astype(f32),
        dup_w.astype(f32),
        ddown.astype(f32),
        smalls[at + 2 * rows_p : at + 2 * rows_p + rows_a],
        dact_a[:, :hq],
        dact_a[:, hq : hq + depth],
        dact_a[:, hq + depth : hq + 2 * depth],
        dact_a[:, hq + 2 * depth :],
        smalls[at + 2 * rows_p + rows_a : at + 2 * rows_p + 2 * rows_a],
        dgu_a[0].astype(f32),
        dgu_a[1].astype(f32),
        ddown_a.astype(f32),
        smalls[:at].reshape(-1, levels),
    )


def solution(mesh):
    return jax.shard_map(
        per_device,
        mesh=mesh,
        in_specs=(
            P(None, ("dp", "noise"), None, None),
            P(None, ("dp", "noise"), None, None),
            P(None, ("dp", "noise")),
            P(None, ("dp", "noise")),
            P(None, "dp"),
            P(None, "dp"),
            P(("dp", "noise")),
            P(("dp", "noise"), None),
            P(("dp", "noise"), None),
            P(("dp", "noise"), None),
            P(("dp", "noise"), None),
            P(("dp", "noise")),
            P(("dp", "noise"), None),
            P(("dp", "noise"), None),
            P(("dp", "noise"), None),
            P(("dp", "noise")),
            P(("dp", "noise"), None),
            P(("dp", "noise"), None),
            P(("dp", "noise"), None),
            P(("dp", "noise"), None),
            P(("dp", "noise")),
            P(("dp", "noise"), None),
            P(("dp", "noise"), None),
            P(("dp", "noise"), None),
            P(("dp", "noise"), None),
            P(None, ("dp", "noise"), None, None),
            P(None, ("dp", "noise"), None, None),
        ),
        out_specs=(
            P(None, ("dp", "noise"), None, None),
            P(None, ("dp", "noise"), None, None),
            P(None, ("dp", "noise"), None, None),
            P(None, ("dp", "noise"), None, None),
            P(("dp", "noise")),
            P(("dp", "noise"), None),
            P(("dp", "noise"), None),
            P(("dp", "noise"), None),
            P(("dp", "noise"), None),
            P(("dp", "noise")),
            P(("dp", "noise"), None),
            P(("dp", "noise"), None),
            P(("dp", "noise"), None),
            P(("dp", "noise")),
            P(("dp", "noise"), None),
            P(("dp", "noise"), None),
            P(("dp", "noise"), None),
            P(("dp", "noise"), None),
            P(("dp", "noise")),
            P(("dp", "noise"), None),
            P(("dp", "noise"), None),
            P(("dp", "noise"), None),
            P(("dp", "noise"), None),
        ),
        check_vma=False,
    )
```

```python
import jax
import jax.numpy as jnp
from jax import lax
from jax.experimental import pallas as pl
from jax.experimental.pallas import tpu as pltpu
from jax.sharding import PartitionSpec as P

EPS = 1e-06
HIGH = lax.Precision.HIGHEST
ALL = ("dp", "noise")
BF = jnp.bfloat16
F32 = jnp.float32
ROOT = 0.7978845608028654
MASKED = -1e30


def normed(rows):
    factor = lax.rsqrt(jnp.mean(rows * rows, axis=-1, keepdims=True) + EPS)
    return (rows * factor, factor)


def norm_back(grad_hidden, normal, factor, gain_mod):
    grad_normal = grad_hidden * gain_mod
    centred = jnp.mean(grad_normal * normal, axis=-1, keepdims=True)
    return factor * (grad_normal - normal * centred)


def flatten(array):
    return array.reshape(-1, array.shape[-1])


def gelu_parts(gate):
    square = gate * gate
    t = jnp.tanh(gate * (ROOT + (ROOT * 0.044715) * square))
    half = 0.5 + 0.5 * t
    slope = half + (gate * (1.0 - t * t)) * ((0.5 * ROOT) + (1.5 * 0.044715 * ROOT) * square)
    return gate * half, slope


def dot(a, b):
    return lax.dot_general(a, b, (((1,), (0,)), ((), ())), preferred_element_type=F32)


def dot_t(a, b):
    return lax.dot_general(a, b, (((1,), (1,)), ((), ())), preferred_element_type=F32)


def dot_w(a, b):
    return lax.dot_general(a, b, (((0,), (0,)), ((), ())), preferred_element_type=F32)


class Line:
    def __init__(self, axes):
        self.axes = axes
        names = (axes,) if isinstance(axes, str) else axes
        self.count, self.me = 1, 0
        for name in names:
            self.count *= lax.axis_size(name)
            self.me = self.me * lax.axis_size(name) + lax.axis_index(name)
        self.bits = list(range(self.count.bit_length() - 1))

    def across(self, x, mask):
        return lax.ppermute(x, self.axes, [(i, i ^ mask) for i in range(self.count)])

    def swap(self, x, bit):
        return self.across(x, 1 << bit)

    def around(self, x, gate=()):
        parts = [self.across(x, far << 1) for far in range(1, self.count // 2)]
        if gate:
            parts = list(after(parts, *gate))
        parts = jnp.stack([x] + parts)
        both = jnp.stack([parts, self.swap(parts, 0)], axis=1)
        return both.reshape((self.count,) + x.shape)

    def home(self, x):
        x = x.reshape((self.count // 2, 2) + x.shape[1:])
        return x[:, 0] + self.swap(x[:, 1], 0)

    def home_end(self, x, gate=()):
        parts = [self.across(x[far], far << 1) for far in range(1, self.count // 2)]
        if gate:
            parts = list(after(parts, *gate))
        return sum((part.astype(F32) for part in parts), x[0].astype(F32))


class Sum:
    def __init__(self, x, dp, line):
        self.x, self.dp, self.line = x, dp, line
        self.rest = x.shape[1:]

    def cores(self):
        x = self.x.reshape((self.dp.count, self.line.count // 2, 2) + self.rest)
        mine = self.line.me % 2
        keep = lax.dynamic_index_in_dim(x, mine, 2, keepdims=False)
        send = lax.dynamic_index_in_dim(x, 1 - mine, 2, keepdims=False)
        self.x = keep + self.line.swap(send, 0)
        return self

    def all_pairs(self, line, me, count, shift, gate):
        mine = lax.dynamic_index_in_dim(self.x, me, 0, keepdims=False).astype(F32)
        parts = []
        for k in range(1, count):
            part = lax.dynamic_index_in_dim(self.x, me ^ k, 0, keepdims=False)
            parts.append(line.across(part, k << shift))
        if gate:
            parts = after(parts, *gate)
        return sum((part.astype(F32) for part in parts), mine)

    def groups(self, gate=()):
        self.x = self.all_pairs(self.dp, self.dp.me, self.dp.count, 0, gate).astype(self.x.dtype)
        return self

    def along(self, gate=()):
        return self.all_pairs(self.line, self.line.me // 2, self.line.count // 2, 1, gate)


def turned(x, me):
    count = x.shape[0]

    def kernel(me_ref, x_ref, out_ref):
        for k in range(count):
            out_ref[me_ref[0] ^ k] = x_ref[k]

    whole = pl.BlockSpec(x.shape, lambda i, me: (0,) * x.ndim, pipeline_mode=pl.Buffered(1))
    return pl.pallas_call(
        kernel,
        grid_spec=pltpu.PrefetchScalarGridSpec(
            num_scalar_prefetch=1, grid=(1,), in_specs=[whole], out_specs=whole
        ),
        out_shape=jax.ShapeDtypeStruct(x.shape, x.dtype),
        compiler_params=params(32, 1),
        name="turn",
    )(me.astype(jnp.int32)[None], x)


def tiles(x, gap, back=None):
    if back is None:
        rows, cols = x.shape
        count = rows // 8 * (cols // 128)
        high = gap // 8
        wide = -(-count // high)
        x = x.reshape(rows // 8, 8, cols // 128, 128).transpose(0, 2, 1, 3).reshape(count, 8, 128)
        x = jnp.pad(x, ((0, high * wide - count), (0, 0), (0, 0)))
        return x.reshape(high, wide, 8, 128).transpose(0, 2, 1, 3).reshape(gap, wide * 128)
    rows, cols = back
    count = rows // 8 * (cols // 128)
    high, wide = gap // 8, x.shape[-1] // 128
    x = x.reshape(-1, high, 8, wide, 128).transpose(0, 1, 3, 2, 4).reshape(-1, high * wide, 8, 128)
    x = x[:, :count].reshape(-1, rows // 8, cols // 128, 8, 128).transpose(0, 1, 3, 2, 4)
    return x.reshape(-1, cols)


def params(megabytes, dims):
    return pltpu.CompilerParams(
        vmem_limit_bytes=megabytes << 20, dimension_semantics=("arbitrary",) * dims
    )


def chained(kernel, at, count):
    def inner(*refs):
        kernel(*refs[:at], *refs[at + count :])

    return inner


def kept(count):
    return [pl.BlockSpec(memory_space=pl.ANY)] * count


def after(values, *others):
    def kernel(*refs):
        pass

    where = pl.BlockSpec(memory_space=pl.ANY)
    return pl.pallas_call(
        kernel,
        in_specs=[where] * (len(values) + len(others)),
        out_specs=[where] * len(values),
        out_shape=[jax.ShapeDtypeStruct(v.shape, v.dtype) for v in values],
        input_output_aliases={i: i for i in range(len(values))},
        name="after",
    )(*values, *others)


def cost(flops, moved, exps=0):
    return pl.CostEstimate(flops=flops, bytes_accessed=moved, transcendentals=exps)


def attend_kernel(step, len_ref, q_ref, k_ref, v_ref, o_ref, lse_ref):
    depth = k_ref.shape[-1]
    q = q_ref[0] * (depth**-0.5)
    s = dot_t(k_ref[0], q.astype(BF))
    ids = lax.broadcasted_iota(jnp.int32, s.shape, 0)
    s = jnp.where(ids < len_ref[step], s, MASKED)
    top = jnp.max(s, axis=0, keepdims=True)
    e = jnp.exp(s - top)
    total = jnp.sum(e, axis=0, keepdims=True)
    p = (e * (1.0 / total)).astype(BF)
    o_ref[0] = dot_w(p, v_ref[0]).astype(BF)
    lse_ref[0, 0] = top + jnp.log(total)


def attend(step, qkv, lens, heads, before=(), gate=()):
    micro, rows, all_width = qkv.shape
    depth = all_width // (heads + 2)
    spec = lambda f: pl.BlockSpec((1, rows, depth), f)

    def kernel(*refs):
        attend_kernel(step, *refs)

    return pl.pallas_call(
        chained(kernel, 4, len(before) + len(gate)),
        grid_spec=pltpu.PrefetchScalarGridSpec(
            num_scalar_prefetch=1,
            grid=(heads,),
            in_specs=[
                spec(lambda h, s: (step, 0, h)),
                spec(lambda h, s: (step, 0, heads)),
                spec(lambda h, s: (step, 0, heads + 1)),
            ]
            + kept(len(before) + len(gate)),
            out_specs=[
                spec(lambda h, s: (step, 0, h)),
                pl.BlockSpec((1, 1, 1, rows), lambda h, s: (step, h, 0, 0)),
            ],
        ),
        out_shape=[
            jax.ShapeDtypeStruct((micro, rows, heads * depth), BF),
            jax.ShapeDtypeStruct((micro, heads, 1, rows), F32),
        ],
        input_output_aliases={4 + i: i for i in range(len(before))},
        compiler_params=params(48, 1),
        cost_estimate=cost(4 * heads * rows * rows * depth, 2 * rows * all_width * 2),
        name="attend",
    )(lens, qkv, qkv, qkv, *before, *gate)


def attend_back_kernel(step, len_ref, q_ref, k_ref, v_ref, do_ref, lse_ref, dq_ref, dk_ref, dv_ref):
    depth = k_ref.shape[-1]
    scale = depth**-0.5

    @pl.when(pl.program_id(0) == 0)
    def _():
        dk_ref[...] = jnp.zeros_like(dk_ref)
        dv_ref[...] = jnp.zeros_like(dv_ref)

    q = (q_ref[0] * scale).astype(BF)
    do = do_ref[0]
    s = dot_t(k_ref[0], q)
    ids = lax.broadcasted_iota(jnp.int32, s.shape, 0)
    p = jnp.where(ids < len_ref[step], jnp.exp(s - lse_ref[0, 0]), 0.0)
    dv_ref[0] += dot(p.astype(BF), do)
    dp = dot_t(v_ref[0], do)
    centre = jnp.sum(p * dp, axis=0, keepdims=True)
    ds = (p * (dp - centre)).astype(BF)
    dk_ref[0] += dot(ds, q)
    dq_ref[0] = (dot_w(ds, k_ref[0]) * scale).astype(BF)


def attend_back(step, qkv, dout, lse, lens, heads, before=(), gate=()):
    micro, rows, all_width = qkv.shape
    depth = all_width // (heads + 2)
    spec = lambda f: pl.BlockSpec((1, rows, depth), f)

    def kernel(*refs):
        attend_back_kernel(step, *refs)

    return pl.pallas_call(
        chained(kernel, 6, len(before) + len(gate)),
        grid_spec=pltpu.PrefetchScalarGridSpec(
            num_scalar_prefetch=1,
            grid=(heads,),
            in_specs=[
                spec(lambda h, s: (step, 0, h)),
                spec(lambda h, s: (step, 0, heads)),
                spec(lambda h, s: (step, 0, heads + 1)),
                spec(lambda h, s: (step, 0, h)),
                pl.BlockSpec((1, 1, 1, rows), lambda h, s: (step, h, 0, 0)),
            ]
            + kept(len(before) + len(gate)),
            out_specs=[
                spec(lambda h, s: (step, 0, h)),
                spec(lambda h, s: (step, 0, 0)),
                spec(lambda h, s: (step, 0, 0)),
            ],
        ),
        out_shape=[
            jax.ShapeDtypeStruct((micro, rows, heads * depth), BF),
            jax.ShapeDtypeStruct((micro, rows, depth), F32),
            jax.ShapeDtypeStruct((micro, rows, depth), F32),
        ],
        input_output_aliases={6 + i: i for i in range(len(before))},
        compiler_params=params(48, 1),
        cost_estimate=cost(10 * heads * rows * rows * depth, 5 * rows * all_width * 2),
        name="attend_back",
    )(lens, qkv, qkv, qkv, dout, lse, *before, *gate)


def feed_kernel(
    o_ref, x_ref, cot_ref, wm_ref, gain_ref, wg_ref, wu_ref, wd_ref, spread_ref,
    out_ref, dx_ref, dmixed_ref, dattn_ref, hw_ref, mid_ref, dgate_ref, dup_ref, dgain_ref,
    h_ref, acc_ref, dh_ref,
):
    at = pl.program_id(0)
    last = pl.num_programs(0) - 1

    @pl.when(at == 0)
    def _():
        x1 = x_ref[...].astype(F32) + dot(o_ref[...], wm_ref[...])
        h = (normed(x1)[0] * gain_ref[...]).astype(BF)
        h_ref[...] = h
        hw_ref[...] = dot(h, spread_ref[...]).astype(BF)
        acc_ref[...] = x1
        dx_ref[...] = x1
        dh_ref[...] = jnp.zeros_like(dh_ref)

    h = h_ref[...]
    dy = cot_ref[...]
    gate = dot(h, wg_ref[...])
    up = dot(h, wu_ref[...])
    dmid = dot_t(dy, wd_ref[...])
    act, slope = gelu_parts(gate)
    mid = (act * up).astype(BF)
    dgate = (dmid * up * slope).astype(BF)
    dup = (dmid * act).astype(BF)
    mid_ref[...] = mid
    dgate_ref[...] = dgate
    dup_ref[...] = dup
    acc_ref[...] += dot(mid, wd_ref[...])
    dh_ref[...] += dot_t(dgate, wg_ref[...]) + dot_t(dup, wu_ref[...])

    @pl.when(at == last)
    def _():
        out_ref[...] = acc_ref[...].astype(BF)
        normal, factor = normed(dx_ref[...])
        dh = dh_ref[...]
        dgain_ref[...] = jnp.sum(dh * normal, axis=0, keepdims=True)
        dx = cot_ref[...].astype(F32) + norm_back(dh, normal, factor, gain_ref[...])
        dx_ref[...] = dx
        dmixed = dx.astype(BF)
        dmixed_ref[...] = dmixed
        dattn_ref[...] = dot_t(dmixed, wm_ref[...]).astype(BF)


def feed(step, micro, o, x, cot, wm, gain, wgu, wd, spread, before=(), gate=()):
    total, width = x.shape
    rows = total // micro
    hq, ff = o.shape[1], wd.shape[0]
    unit = 512
    chunks = ff // unit
    once = dict(pipeline_mode=pl.Buffered(1))
    row = lambda w: pl.BlockSpec((rows, w), lambda i: (step, 0), **once)
    col = lambda f: pl.BlockSpec((rows, unit), f)
    whole = lambda a: pl.BlockSpec(a.shape, lambda i: (0, 0), **once)
    out = lambda w, t: jax.ShapeDtypeStruct((total, w), t)
    wide = spread.shape[1]
    kernel = chained(feed_kernel, 9, len(before) + len(gate))
    return pl.pallas_call(
        kernel,
        grid=(chunks,),
        in_specs=[row(hq), row(width), row(width), whole(wm), whole(gain)]
        + [
            pl.BlockSpec((width, unit), lambda i: (0, i)),
            pl.BlockSpec((width, unit), lambda i: (0, chunks + i)),
            pl.BlockSpec((unit, width), lambda i: (i, 0)),
            whole(spread),
        ]
        + kept(len(before) + len(gate)),
        out_specs=[row(width), row(width), row(width), row(hq), row(wide)]
        + [col(lambda i: (step, i))] * 3
        + [pl.BlockSpec((1, width), lambda i: (0, 0))],
        out_shape=[
            out(width, BF), out(width, F32), out(width, BF), out(hq, BF), out(wide, BF),
            out(ff, BF), out(ff, BF), out(ff, BF), jax.ShapeDtypeStruct((1, width), F32),
        ],
        scratch_shapes=[
            pltpu.VMEM((rows, width), BF),
            pltpu.VMEM((rows, width), F32),
            pltpu.VMEM((rows, width), F32),
        ],
        input_output_aliases={9 + i: i for i in range(len(before))},
        compiler_params=params(60, 1),
        cost_estimate=cost(rows * (12 * width * ff + 4 * width * hq), rows * ff * 8 + wgu.size * 3),
        name="feed",
    )(o, x, cot, wm, gain, wgu, wgu, wd, spread, *before, *gate)


def weight_grad_kernel(x_ref, *refs):
    *g_refs, out_ref, turned_ref = refs
    at = pl.program_id(0)

    @pl.when(at == 0)
    def _():
        turned_ref[...] = x_ref[...].T

    each = pl.num_programs(0) // len(g_refs)
    for i, g_ref in enumerate(g_refs):

        @pl.when(at // each == i)
        def _():
            out_ref[...] = dot(turned_ref[...], g_ref[...]).astype(BF)


def weight_grad(x, grads, unit, columns=None, gate=()):
    rows, width = x.shape
    each = grads[0].shape[1] // unit
    count = each * len(grads)
    columns = columns or count * unit

    def place(i):
        return pl.BlockSpec(
            (rows, unit), lambda at: (0, jnp.clip(at - i * each, 0, each - 1))
        )

    return pl.pallas_call(
        chained(weight_grad_kernel, 1 + len(grads), len(gate)),
        grid=(count,),
        in_specs=[
            pl.BlockSpec((rows, width), lambda at: (0, 0), pipeline_mode=pl.Buffered(1))
        ]
        + [place(i) for i in range(len(grads))]
        + kept(len(gate)),
        out_specs=pl.BlockSpec((width, unit), lambda at: (0, at)),
        out_shape=jax.ShapeDtypeStruct((width, columns), BF),
        scratch_shapes=[pltpu.VMEM((width, rows), BF)],
        compiler_params=params(48, 1),
        cost_estimate=cost(2 * rows * width * count * unit, 2 * rows * (width + count * unit)),
        name="weight_grad",
    )(x, *grads, *gate)


def stack_heads(x, heads):
    depth = x.shape[-1] // heads
    return jnp.concatenate([x[:, h * depth : (h + 1) * depth] for h in range(heads)], axis=0)


def own_scores(heads, scale, length, seg_len, qkv_ref, k_ref):
    depth = k_ref.shape[-1]
    qkv = qkv_ref[0, 0].astype(F32)
    q = (stack_heads(qkv[:, : heads * depth], heads) * scale).astype(BF)
    near_k = qkv[:, heads * depth : (heads + 1) * depth].astype(BF)
    near_v = qkv[:, (heads + 1) * depth :].astype(BF)
    far = dot_t(k_ref[0], q)
    near = dot_t(near_k, q)
    far_ok = lax.broadcasted_iota(jnp.int32, far.shape, 0) < length
    near_ok = lax.broadcasted_iota(jnp.int32, near.shape, 0) < seg_len
    return q, near_k, near_v, jnp.where(far_ok, far, MASKED), jnp.where(near_ok, near, MASKED)


def own_kernel(heads, seg_len, own_ref, len_ref, qkv_ref, k_ref, v_ref, o_ref, lse_ref):
    m, c = pl.program_id(0), pl.program_id(1)
    mine = own_ref[m * pl.num_programs(1) + c] == 1
    depth = k_ref.shape[-1]
    rows = qkv_ref.shape[2]

    @pl.when(mine)
    def _():
        q, near_k, near_v, far, near = own_scores(
            heads, depth**-0.5, len_ref[m], seg_len, qkv_ref, k_ref
        )
        top = jnp.maximum(
            jnp.max(far, axis=0, keepdims=True), jnp.max(near, axis=0, keepdims=True)
        )
        far, near = jnp.exp(far - top), jnp.exp(near - top)
        total = jnp.sum(far, axis=0, keepdims=True) + jnp.sum(near, axis=0, keepdims=True)
        part = 1.0 / total
        o = dot_w((far * part).astype(BF), v_ref[0]) + dot_w((near * part).astype(BF), near_v)
        for h in range(heads):
            o_ref[0, 0, :, h * depth : (h + 1) * depth] = o[h * rows : (h + 1) * rows].astype(BF)
        lse_ref[0, 0] = top + jnp.log(total)

    @pl.when(jnp.logical_not(mine))
    def _():
        o_ref[...] = jnp.zeros_like(o_ref)
        lse_ref[...] = jnp.zeros_like(lse_ref)


def own_attend(seg_qkv, qkv, own, lens, heads, seg_len):
    n, micro, rows, all_width = seg_qkv.shape
    depth = all_width // (heads + 2)
    prefix = qkv.shape[1]
    seg = lambda w: pl.BlockSpec((1, 1, rows, w), lambda m, c, a, b: (c, m, 0, 0))
    stat = pl.BlockSpec((1, 1, 1, heads * rows), lambda m, c, a, b: (c, m, 0, 0))

    def kernel(*refs):
        own_kernel(heads, seg_len, *refs)

    return pl.pallas_call(
        kernel,
        grid_spec=pltpu.PrefetchScalarGridSpec(
            num_scalar_prefetch=2,
            grid=(micro, n),
            in_specs=[
                seg(all_width),
                pl.BlockSpec((1, prefix, depth), lambda m, c, a, b: (m, 0, heads)),
                pl.BlockSpec((1, prefix, depth), lambda m, c, a, b: (m, 0, heads + 1)),
            ],
            out_specs=[seg(heads * depth), stat],
        ),
        out_shape=[
            jax.ShapeDtypeStruct((n, micro, rows, heads * depth), BF),
            jax.ShapeDtypeStruct((n, micro, 1, heads * rows), F32),
        ],
        compiler_params=params(32, 2),
        cost_estimate=cost(4 * 2 * micro * heads * rows * prefix * depth, 4 * seg_qkv.size),
        name="own_attend",
    )(own, lens, seg_qkv, qkv, qkv)


def own_back_kernel(
    heads, seg_len, own_ref, len_ref, qkv_ref, k_ref, v_ref, do_ref, lse_ref, dqkv_ref, dk_ref, dv_ref
):
    m, c = pl.program_id(0), pl.program_id(1)
    mine = own_ref[m * pl.num_programs(1) + c] == 1
    depth = k_ref.shape[-1]
    rows = qkv_ref.shape[2]
    scale = depth**-0.5

    @pl.when(c == 0)
    def _():
        dk_ref[...] = jnp.zeros_like(dk_ref)
        dv_ref[...] = jnp.zeros_like(dv_ref)

    @pl.when(mine)
    def _():
        q, near_k, near_v, far, near = own_scores(heads, scale, len_ref[m], seg_len, qkv_ref, k_ref)
        far, near = jnp.exp(far - lse_ref[0, 0]), jnp.exp(near - lse_ref[0, 0])
        do = stack_heads(do_ref[0, 0].astype(F32), heads).astype(BF)
        dv_ref[0] += dot(far.astype(BF), do)
        dfar, dnear = dot_t(v_ref[0], do), dot_t(near_v, do)
        centre = jnp.sum(far * dfar, axis=0, keepdims=True)
        centre = centre + jnp.sum(near * dnear, axis=0, keepdims=True)
        sfar = (far * (dfar - centre)).astype(BF)
        snear = (near * (dnear - centre)).astype(BF)
        dk_ref[0] += dot(sfar, q)
        dq = (dot_w(sfar, k_ref[0]) + dot_w(snear, near_k)) * scale
        for h in range(heads):
            dqkv_ref[0, 0, :, h * depth : (h + 1) * depth] = dq[h * rows : (h + 1) * rows].astype(BF)
        dqkv_ref[0, 0, :, heads * depth : (heads + 1) * depth] = dot(snear, q).astype(BF)
        dqkv_ref[0, 0, :, (heads + 1) * depth :] = dot(near.astype(BF), do).astype(BF)

    @pl.when(jnp.logical_not(mine))
    def _():
        dqkv_ref[...] = jnp.zeros_like(dqkv_ref)


def own_back(seg_qkv, qkv, dout, lse, own, lens, heads, seg_len):
    n, micro, rows, all_width = seg_qkv.shape
    depth = all_width // (heads + 2)
    prefix = qkv.shape[1]
    seg = lambda w: pl.BlockSpec((1, 1, rows, w), lambda m, c, a, b: (c, m, 0, 0))
    item = lambda i: pl.BlockSpec((1, prefix, depth), lambda m, c, a, b: (m, 0, i))

    def kernel(*refs):
        own_back_kernel(heads, seg_len, *refs)

    return pl.pallas_call(
        kernel,
        grid_spec=pltpu.PrefetchScalarGridSpec(
            num_scalar_prefetch=2,
            grid=(micro, n),
            in_specs=[
                seg(all_width),
                item(heads),
                item(heads + 1),
                seg(heads * depth),
                pl.BlockSpec((1, 1, 1, heads * rows), lambda m, c, a, b: (c, m, 0, 0)),
            ],
            out_specs=[seg(all_width), item(0), item(0)],
        ),
        out_shape=[
            jax.ShapeDtypeStruct((n, micro, rows, all_width), BF),
            jax.ShapeDtypeStruct((micro, prefix, depth), F32),
            jax.ShapeDtypeStruct((micro, prefix, depth), F32),
        ],
        compiler_params=params(32, 2),
        cost_estimate=cost(10 * 2 * micro * heads * rows * prefix * depth, 8 * seg_qkv.size),
        name="own_back",
    )(own, lens, seg_qkv, qkv, qkv, dout, lse)


def per_device(
    prefix_rows,
    action_rows,
    segment_item,
    segment_time,
    item_weight,
    prefix_len,
    vlm_prenorm,
    vlm_query,
    vlm_key,
    vlm_value,
    vlm_mixer,
    vlm_midnorm,
    vlm_gate,
    vlm_expand,
    vlm_down,
    act_prenorm,
    act_query,
    act_key,
    act_value,
    act_mixer,
    act_midnorm,
    act_gate,
    act_expand,
    act_down,
    time_scales,
    cot_prefix,
    cot_action,
):
    micro, items, prefix, width = prefix_rows.shape
    seg_len, wide = action_rows.shape[2:]
    groups, n = lax.axis_size("dp"), lax.axis_size("noise")
    depth, hq = vlm_key.shape[1], vlm_query.shape[1]
    heads = hq // depth
    joint = hq + 2 * depth
    ff, ffa = vlm_gate.shape[1], act_gate.shape[1]
    levels = time_scales.shape[1]
    rows_p, rows_a = vlm_query.shape[0], act_query.shape[0]
    here = lax.axis_index("noise")
    every, line = Line(ALL), Line("noise")
    total = every.count
    dp = Line("dp")
    slot = -(-(seg_len + 1) // 8) * 8
    block = micro * slot

    lanes = lambda x, w: jnp.pad(x, ((0, 0), (0, w - x.shape[1])))
    gap = -(-rows_p // 8) * 8
    taller = lambda x: jnp.pad(x, ((0, gap - rows_p), (0, 0)))
    rows_m = vlm_mixer.shape[0]
    unit = act_down.shape[0]
    part = groups * unit

    item, time = segment_item[:, 0], segment_time[:, 0]
    spare = jnp.zeros((micro, slot - seg_len, wide), BF)
    tags = spare.at[:, 0, 0].set(item.astype(BF)).at[:, 0, 1].set(time.astype(BF))
    action_in = jnp.concatenate([action_rows[:, 0], tags], axis=1)
    hot = item[:, None] == jnp.arange(prefix_len.shape[1])[None, :]
    weight = (jnp.sum(jnp.where(hot, item_weight, 0), axis=1) + 1).astype(F32) / 8.0
    grad_action = cot_action[:, 0].astype(F32) * weight[:, None, None]
    grad_action = jnp.pad(grad_action, ((0, 0), (0, slot - seg_len), (0, 0)))

    pre_pack = jnp.concatenate(
        [
            vlm_query,
            vlm_key,
            vlm_value,
            lanes(jnp.stack([vlm_prenorm, vlm_midnorm], axis=1), 128),
        ],
        axis=1,
    )
    act_small = [act_prenorm[:, None], act_midnorm[:, None], time_scales.reshape(rows_a, -1)]
    act_pack = [act_query, act_key, act_value, lanes(jnp.concatenate(act_small, axis=1), 128)]
    act_pack = jnp.concatenate(act_pack, axis=1)
    first = [act_pack, taller(pre_pack), lanes(tiles(act_mixer, gap), act_pack.shape[1])]
    first = lax.all_gather(jnp.concatenate(first, axis=0), ALL, axis=0)
    act_a = first[:, :rows_a].reshape(total * rows_a, -1)
    pre_a = first[:, rows_a : rows_a + gap].reshape(total * gap, -1)
    suf_mixer = first[:, rows_a + gap :]

    fold = jnp.concatenate([vlm_mixer, vlm_down], axis=0)
    second = [taller(vlm_gate), taller(vlm_expand), tiles(fold, gap)]
    second = lax.all_gather(jnp.concatenate(second, axis=1), ALL, axis=0)

    cols = jnp.stack([act_gate, act_expand]).reshape(2, rows_a, groups, n, unit)
    cols = cols.transpose(3, 0, 1, 2, 4).reshape(n, 2, rows_a, part)
    cols = lax.all_to_all(cols, "noise", 0, 0, tiled=True)
    cols = cols.transpose(0, 2, 1, 3).reshape(n * rows_a, 2 * part)
    hidden_w = jnp.concatenate([cols, act_down.reshape(-1, 2 * part)], axis=0)
    hidden_w = jnp.stack([hidden_w] + [dp.across(hidden_w, k) for k in range(1, groups)])
    hidden_w = turned(hidden_w, dp.me)
    gu_w = hidden_w[:, : n * rows_a].reshape(-1, 2 * part)
    down_w = hidden_w[:, n * rows_a :].reshape(part, wide)
    dy_all = line.around(grad_action.astype(BF).reshape(block, wide)).reshape(-1, wide)

    seg_all = line.around(action_in)

    places = jnp.arange(total * gap)
    spread = (places // gap * rows_p + places % gap)[None, :] == jnp.arange(width)[:, None]
    spread = (spread & (places % gap < rows_p)[None, :]).astype(BF)
    pre_a = dot(spread, pre_a).astype(BF)
    pre_qkv = pre_a[:, :joint]
    pre_gain = pre_a[:, joint].astype(F32)
    pre_midgain = pre_a[:, joint + 1].astype(F32)
    suf_qkv = act_a[:, :joint]
    small = act_a[:, joint:].astype(F32)
    suf_gain, suf_midgain = small[:, 0], small[:, 1]
    table = small[:, 2 : 2 + time_scales.size // rows_a].reshape(2 * wide, levels)

    times = seg_all[:, :, seg_len, 1].astype(jnp.int32)
    own = (seg_all[:, :, seg_len, 0].astype(jnp.int32) == here).astype(jnp.int32)
    own = own.T.reshape(-1)
    is_row = (jnp.arange(slot) < seg_len)[:, None]
    hots = (times[..., None] == jnp.arange(levels)).astype(F32)
    mods = jnp.einsum("nmt,jt->nmj", hots, table, precision=HIGH)
    mod1_all = mods[:, :, None, :wide]
    mod2 = mods[0, :, None, wide:]
    an1, as1 = normed(jnp.where(is_row, seg_all, 0).astype(F32))
    ah1 = flatten((an1 * suf_gain * mod1_all).astype(BF))
    seg_qkv = dot(ah1, suf_qkv).astype(BF).reshape(n, micro, slot, joint)

    x = prefix_rows[:, 0]
    n1, s1 = normed(x.astype(F32))
    h1 = flatten((n1 * pre_gain).astype(BF))
    qkv = dot(h1, pre_qkv).astype(BF).reshape(micro, prefix, joint)
    lens = lax.dynamic_slice_in_dim(prefix_len, here, 1, axis=1)[:, 0]

    oa, lse_a = own_attend(seg_qkv, qkv, own, lens, heads, seg_len)

    outs = attend(0, qkv, lens, heads, (), (oa,))
    oa = line.home(oa.reshape(n, block, hq))
    outs = attend(1, qkv, lens, heads, outs, (oa,))
    o, lse = outs
    oa = line.home_end(oa, (o,)).astype(BF)
    suf_mixer = suf_mixer[..., : tiles(act_mixer, gap).shape[1]]
    suf_mixer = tiles(suf_mixer, gap, act_mixer.shape)
    a1 = jnp.where(is_row, action_in, 0).astype(F32) + dot(oa, suf_mixer).reshape(micro, slot, wide)
    an2, as2 = normed(a1)
    ah2 = (an2 * suf_midgain * mod2).astype(BF).reshape(block, wide)

    h_all = line.around(ah2).reshape(n * block, wide)
    gu = dot(h_all, gu_w)
    gate_a, up_a = gu[:, :part], gu[:, part:]
    act_g, slope_g = gelu_parts(gate_a)
    mid_a = (act_g * up_a).astype(BF)
    dmid_a = dot_t(dy_all, down_w)
    dgu = jnp.concatenate(
        [(dmid_a * up_a * slope_g).astype(BF), (dmid_a * act_g).astype(BF)], axis=1
    )
    grad_late = line.home(dot_t(dgu, gu_w).astype(BF).reshape(n, block, wide))
    out_a = line.home(dot(mid_a, down_w).astype(BF).reshape(n, block, wide))
    dff = jnp.concatenate(
        [
            dot_w(h_all, dgu).astype(BF).reshape(groups, n * rows_a, 2 * part),
            dot_w(mid_a, dy_all).astype(BF).reshape(groups, -1, 2 * part),
        ],
        axis=1,
    )
    dff = dff.reshape(-1, 2 * part)
    dff = lax.psum_scatter(dff, "dp", scatter_dimension=0, tiled=True)

    pre_gu = dot(spread, second[..., : 2 * ff].reshape(total * gap, -1)).astype(BF)
    fold = tiles(second[..., 2 * ff :], gap, fold.shape).reshape(total, -1, width)
    pre_mixer = fold[:, :rows_m].reshape(hq, width)
    pre_down = fold[:, rows_m:].reshape(ff, width)
    cot = cot_prefix.reshape(micro * prefix, width)

    def feed_half(step, outs, gate):
        return feed(
            step, micro, o.reshape(-1, hq), x.reshape(-1, width), cot,
            pre_mixer, pre_midgain[None], pre_gu, pre_down, spread, outs, gate,
        )

    outs = feed_half(0, (), (grad_late,))
    pre_dmid = outs[-1]
    grad_late = line.home_end(grad_late, (outs[0],)).reshape(micro, slot, wide)
    late_back = grad_late * an2
    suf_dmid = jnp.sum(late_back * mod2, axis=(0, 1))
    dmod2 = jnp.sum(late_back * suf_midgain, axis=1)
    da1 = grad_action + norm_back(grad_late, an2, as2, suf_midgain * mod2)
    dmixed_a = da1.astype(BF).reshape(block, wide)
    dattn_a = dot_t(dmixed_a, suf_mixer).astype(BF)
    outs = feed_half(1, outs[:-1], (dattn_a,))
    pre_dmid = pre_dmid + outs[-1]
    prefix_out, dx1, dmixed, dattn, h2, mid, dgate, dup = outs[:-1]
    dattn_all = line.around(dattn_a, (dx1,)).reshape(n, micro, slot, hq)

    dmd_w = jnp.concatenate(
        [
            weight_grad(o.reshape(-1, hq), [dmixed], width).reshape(total, rows_m, width),
            weight_grad(mid, [cot], width, gate=(dx1,)).reshape(total, -1, width),
        ],
        axis=1,
    )
    grads = [dmd_w, dot_w(oa, dmixed_a).astype(BF).reshape(total, rows_a, -1)]
    grads = [jax.vmap(lambda g: tiles(g, gap))(g) for g in grads]
    cut = grads[0].shape[-1]
    grads = jnp.concatenate(grads, axis=-1)
    grads_sum = lax.psum_scatter(grads, ALL, scatter_dimension=0)
    dmd_w = tiles(grads_sum[:, :cut], gap, dmd_w.shape[1:])
    dam_w = tiles(grads_sum[:, cut:], gap, (rows_a, wide))

    dseg, far_dk, far_dv = own_back(seg_qkv, qkv, dattn_all, lse_a, own, lens, heads, seg_len)
    dseg = dseg.reshape(n * block, joint)
    act_sum = Sum(dot_w(ah1, dseg).astype(BF).reshape(total, rows_a, -1), dp, line).cores()

    big_w = weight_grad(h2, [dgate, dup], 512, gate=(act_sum.x, grads))
    big_sum = Sum(big_w.reshape(total, gap, -1), dp, line).cores()
    dattn = dattn.reshape(micro, prefix, hq)
    outs = attend_back(0, qkv, dattn, lse, lens, heads, (), (big_w,))
    act_sum.groups((outs[0],))
    outs = attend_back(1, qkv, dattn, lse, lens, heads, outs, (big_sum.x, act_sum.x))
    dq, dk, dv = outs
    big_sum.groups((dq,))
    dkv = jnp.concatenate([(dk + far_dk).astype(BF), (dv + far_dv).astype(BF)], axis=-1)
    dqkv = jnp.concatenate([dq, dkv], axis=-1).reshape(-1, joint)
    h1_wide = dot(h1, spread).astype(BF)
    pre_sum = weight_grad(h1_wide, [dqkv], 512).reshape(total, gap, -1)
    pre_sum = Sum(pre_sum, dp, line).cores()

    dah1 = dot_t(dseg, suf_qkv).reshape(n, micro, slot, wide)
    first_back = dah1 * an1
    suf_dgain = jnp.sum(first_back * mod1_all, axis=(0, 1, 2))
    dmod1 = jnp.sum(first_back * suf_gain, axis=2)
    back = norm_back(dah1, an1, as1, suf_gain * mod1_all).astype(BF).reshape(n, block, wide)
    back = line.home_end(line.home(back)).reshape(micro, slot, wide)
    out_a = line.home_end(out_a).reshape(micro, slot, wide)
    action_out = (a1 + out_a)[:, :seg_len].astype(BF)
    action_grad = (da1 + back)[:, :seg_len]
    dtable = jnp.concatenate(
        [
            jnp.einsum("nmj,nmt->jt", dmod1, hots, precision=HIGH),
            jnp.einsum("mj,mt->jt", dmod2, hots[0], precision=HIGH),
        ],
        axis=0,
    )
    dh1 = dot_t(dqkv, pre_qkv).reshape(micro, prefix, width)
    pre_dgain = jnp.sum(dh1 * n1, axis=(0, 1))
    prefix_grad = dx1.reshape(micro, prefix, width) + norm_back(dh1, n1, s1, pre_gain)

    ddown_a = dff[n * rows_a :].reshape(unit, wide)
    dgu_a = dff[: n * rows_a].reshape(n, rows_a, 2 * part)
    dgu_a = lax.all_to_all(dgu_a, "noise", 0, 0, tiled=True)
    dgu_a = dgu_a.reshape(n, rows_a, 2, groups, unit).transpose(2, 1, 3, 0, 4)
    dgu_a = dgu_a.reshape(2, rows_a, ffa)
    smalls = jnp.concatenate(
        [
            dtable.reshape(total, -1),
            pre_dgain.reshape(total, rows_p),
            pre_dmid.reshape(total, rows_p),
            suf_dgain.reshape(total, rows_a),
            suf_dmid.reshape(total, rows_a),
        ],
        axis=1,
    )
    smalls = lanes(smalls, -(-smalls.shape[1] // 128) * 128).reshape(total, -1, 128)
    small_sum = Sum(smalls, dp, line)
    smalls = small_sum.cores().groups().along().reshape(-1)
    act_g = act_sum.along()
    big_g = big_sum.along()[:rows_p]
    pre_g = pre_sum.groups().along()[:rows_p]
    at = [dtable.size // total]
    for size in (rows_p, rows_p, rows_a, rows_a):
        at.append(at[-1] + size)
    return (
        prefix_out.reshape(prefix_rows.shape),
        action_out[:, None],
        prefix_grad[:, None],
        action_grad[:, None],
        smalls[at[0] : at[1]],
        pre_g[:, :hq],
        pre_g[:, hq : hq + depth],
        pre_g[:, hq + depth :],
        dmd_w[:rows_m].astype(F32),
        smalls[at[1] : at[2]],
        big_g[:, :ff],
        big_g[:, ff:],
        dmd_w[rows_m:].astype(F32),
        smalls[at[2] : at[3]],
        act_g[:, :hq],
        act_g[:, hq : hq + depth],
        act_g[:, hq + depth :],
        dam_w.astype(F32),
        smalls[at[3] : at[4]],
        dgu_a[0].astype(F32),
        dgu_a[1].astype(F32),
        ddown_a.astype(F32),
        smalls[: at[0]].reshape(-1, levels),
    )


def solution(mesh):
    return jax.shard_map(
        per_device,
        mesh=mesh,
        in_specs=(
            P(None, ("dp", "noise"), None, None),
            P(None, ("dp", "noise"), None, None),
            P(None, ("dp", "noise")),
            P(None, ("dp", "noise")),
            P(None, "dp"),
            P(None, "dp"),
            P(("dp", "noise")),
            P(("dp", "noise"), None),
            P(("dp", "noise"), None),
            P(("dp", "noise"), None),
            P(("dp", "noise"), None),
            P(("dp", "noise")),
            P(("dp", "noise"), None),
            P(("dp", "noise"), None),
            P(("dp", "noise"), None),
            P(("dp", "noise")),
            P(("dp", "noise"), None),
            P(("dp", "noise"), None),
            P(("dp", "noise"), None),
            P(("dp", "noise"), None),
            P(("dp", "noise")),
            P(("dp", "noise"), None),
            P(("dp", "noise"), None),
            P(("dp", "noise"), None),
            P(("dp", "noise"), None),
            P(None, ("dp", "noise"), None, None),
            P(None, ("dp", "noise"), None, None),
        ),
        out_specs=(
            P(None, ("dp", "noise"), None, None),
            P(None, ("dp", "noise"), None, None),
            P(None, ("dp", "noise"), None, None),
            P(None, ("dp", "noise"), None, None),
            P(("dp", "noise")),
            P(("dp", "noise"), None),
            P(("dp", "noise"), None),
            P(("dp", "noise"), None),
            P(("dp", "noise"), None),
            P(("dp", "noise")),
            P(("dp", "noise"), None),
            P(("dp", "noise"), None),
            P(("dp", "noise"), None),
            P(("dp", "noise")),
            P(("dp", "noise"), None),
            P(("dp", "noise"), None),
            P(("dp", "noise"), None),
            P(("dp", "noise"), None),
            P(("dp", "noise")),
            P(("dp", "noise"), None),
            P(("dp", "noise"), None),
            P(("dp", "noise"), None),
            P(("dp", "noise"), None),
        ),
        check_vma=False,
    )
```

```python
import jax
import jax.numpy as jnp
from jax import lax
from jax.experimental import pallas as pl
from jax.experimental.pallas import tpu as pltpu
from jax.sharding import PartitionSpec as P

EPS = 1e-06
HIGH = lax.Precision.HIGHEST
ALL = ("dp", "noise")
BF = jnp.bfloat16
F32 = jnp.float32
ROOT = 0.7978845608028654
MASKED = -1e30


def normed(rows):
    factor = lax.rsqrt(jnp.mean(rows * rows, axis=-1, keepdims=True) + EPS)
    return (rows * factor, factor)


def norm_back(grad_hidden, normal, factor, gain_mod):
    grad_normal = grad_hidden * gain_mod
    centred = jnp.mean(grad_normal * normal, axis=-1, keepdims=True)
    return factor * (grad_normal - normal * centred)


def flatten(array):
    return array.reshape(-1, array.shape[-1])


def gelu_parts(gate):
    square = gate * gate
    t = jnp.tanh(gate * (ROOT + (ROOT * 0.044715) * square))
    half = 0.5 + 0.5 * t
    slope = half + (gate * (1.0 - t * t)) * ((0.5 * ROOT) + (1.5 * 0.044715 * ROOT) * square)
    return gate * half, slope


def dot(a, b):
    return lax.dot_general(a, b, (((1,), (0,)), ((), ())), preferred_element_type=F32)


def dot_t(a, b):
    return lax.dot_general(a, b, (((1,), (1,)), ((), ())), preferred_element_type=F32)


def dot_w(a, b):
    return lax.dot_general(a, b, (((0,), (0,)), ((), ())), preferred_element_type=F32)


class Line:
    def __init__(self, axes):
        self.axes = axes
        names = (axes,) if isinstance(axes, str) else axes
        self.count, self.me = 1, 0
        for name in names:
            self.count *= lax.axis_size(name)
            self.me = self.me * lax.axis_size(name) + lax.axis_index(name)
        self.bits = list(range(self.count.bit_length() - 1))

    def across(self, x, mask):
        return lax.ppermute(x, self.axes, [(i, i ^ mask) for i in range(self.count)])

    def swap(self, x, bit):
        return self.across(x, 1 << bit)

    def around(self, x, gate=()):
        parts = [self.across(x, far << 1) for far in range(1, self.count // 2)]
        if gate:
            parts = list(after(parts, *gate))
        parts = jnp.stack([x] + parts)
        both = jnp.stack([parts, self.swap(parts, 0)], axis=1)
        return both.reshape((self.count,) + x.shape)

    def home(self, x):
        x = x.reshape((self.count // 2, 2) + x.shape[1:])
        return x[:, 0] + self.swap(x[:, 1], 0)

    def home_end(self, x, gate=()):
        parts = [self.across(x[far], far << 1) for far in range(1, self.count // 2)]
        if gate:
            parts = list(after(parts, *gate))
        return sum((part.astype(F32) for part in parts), x[0].astype(F32))


def joint(jobs, *gate):
    return list(after([line.across(x, mask) for line, x, mask in jobs], *gate))


def fetch(x, rows, dp, line, beside):
    far, count = line.count // 2, dp.count
    *got, more = joint([(line, x, k << 1) for k in range(1, far)] + [(line, rows, 2)])
    near = jnp.stack([x] + got)
    rows = jnp.stack([rows, more])
    jobs = [(dp, near, k) for k in range(1, count)]
    for bit in range(2, far.bit_length()):
        more = line.across(rows, 1 << bit)
        if bit + 1 < far.bit_length():
            rows = jnp.concatenate([rows, more])
    done = beside(near)
    got = [line.across(x, mask) for line, x, mask in jobs]
    *got, more, done = after(got + [more, done])
    same = jnp.stack([near] + got)
    rows = jnp.concatenate([rows, more])
    other, more = joint([(line, same, 1), (line, rows, 1)])
    rows = jnp.stack([rows, more], axis=1).reshape((line.count,) + rows.shape[1:])

    def kernel(me_ref, same_ref, other_ref, out_ref):
        for kd in range(count):
            for kz in range(far):
                at = (me_ref[0] ^ kd) * line.count + (me_ref[1] ^ (2 * kz))
                out_ref[at] = same_ref[kd, kz]
                out_ref[at ^ 1] = other_ref[kd, kz]

    def whole(a):
        return pl.BlockSpec(a, lambda i, me: (0,) * len(a), pipeline_mode=pl.Buffered(1))

    shape = (count * line.count,) + x.shape
    me = jnp.stack([dp.me, line.me]).astype(jnp.int32)
    return pl.pallas_call(
        kernel,
        grid_spec=pltpu.PrefetchScalarGridSpec(
            num_scalar_prefetch=1,
            grid=(1,),
            in_specs=[whole(same.shape)] * 2,
            out_specs=whole(shape),
        ),
        out_shape=jax.ShapeDtypeStruct(shape, x.dtype),
        compiler_params=params(48, 1),
        name="settle",
    )(me, same, other), rows, done


class Sum:
    def __init__(self, x, dp, line):
        self.x, self.dp, self.line = x, dp, line
        self.rest = x.shape[1:]
        self.bits = list(range(1, line.count.bit_length() - 1))

    def half(self, lead, bit, tail):
        x = self.x.reshape(lead + (2,) + tail + self.rest)
        mine = (self.line.me >> bit) & 1
        self.x = lax.dynamic_index_in_dim(x, mine, len(lead), keepdims=False)
        send = lax.dynamic_index_in_dim(x, 1 - mine, len(lead), keepdims=False)
        return [(self.line, send, 1 << bit)]

    def cores(self):
        return self.half((self.dp.count, self.line.count // 2), 0, ())

    def groups(self):
        take = lambda k: lax.dynamic_index_in_dim(self.x, self.dp.me ^ k, 0, keepdims=False)
        jobs = [(self.dp, take(k), k) for k in range(1, self.dp.count)]
        self.x = take(0)
        return jobs

    def along(self):
        far = self.x.shape[0] if self.x.ndim > len(self.rest) else 1
        return self.half((far // 2,), self.bits.pop(0), ())

    def take(self, got):
        kind = self.x.dtype
        self.x = sum((x.astype(F32) for x in got), self.x.astype(F32)).astype(kind)

    def result(self):
        while self.bits:
            self.take([line.across(x, mask) for line, x, mask in self.along()])
        return self.x.reshape(self.rest).astype(F32)


def turned(x, me):
    count = x.shape[0]

    def kernel(me_ref, x_ref, out_ref):
        for k in range(count):
            out_ref[me_ref[0] ^ k] = x_ref[k]

    whole = pl.BlockSpec(x.shape, lambda i, me: (0,) * x.ndim, pipeline_mode=pl.Buffered(1))
    return pl.pallas_call(
        kernel,
        grid_spec=pltpu.PrefetchScalarGridSpec(
            num_scalar_prefetch=1, grid=(1,), in_specs=[whole], out_specs=whole
        ),
        out_shape=jax.ShapeDtypeStruct(x.shape, x.dtype),
        compiler_params=params(32, 1),
        name="turn",
    )(me.astype(jnp.int32)[None], x)


def tiles(x, gap, back=None):
    if back is None:
        rows, cols = x.shape
        count = rows // 8 * (cols // 128)
        high = gap // 8
        wide = -(-count // high)
        x = x.reshape(rows // 8, 8, cols // 128, 128).transpose(0, 2, 1, 3).reshape(count, 8, 128)
        x = jnp.pad(x, ((0, high * wide - count), (0, 0), (0, 0)))
        return x.reshape(high, wide, 8, 128).transpose(0, 2, 1, 3).reshape(gap, wide * 128)
    rows, cols = back
    count = rows // 8 * (cols // 128)
    high, wide = gap // 8, x.shape[-1] // 128
    x = x.reshape(-1, high, 8, wide, 128).transpose(0, 1, 3, 2, 4).reshape(-1, high * wide, 8, 128)
    x = x[:, :count].reshape(-1, rows // 8, cols // 128, 8, 128).transpose(0, 1, 3, 2, 4)
    return x.reshape(-1, cols)


def params(megabytes, dims):
    return pltpu.CompilerParams(
        vmem_limit_bytes=megabytes << 20, dimension_semantics=("arbitrary",) * dims
    )


def chained(kernel, at, count):
    def inner(*refs):
        kernel(*refs[:at], *refs[at + count :])

    return inner


def kept(count):
    return [pl.BlockSpec(memory_space=pl.ANY)] * count


def after(values, *others):
    def kernel(*refs):
        pass

    where = pl.BlockSpec(memory_space=pl.ANY)
    return pl.pallas_call(
        kernel,
        in_specs=[where] * (len(values) + len(others)),
        out_specs=[where] * len(values),
        out_shape=[jax.ShapeDtypeStruct(v.shape, v.dtype) for v in values],
        input_output_aliases={i: i for i in range(len(values))},
        name="after",
    )(*values, *others)


def cost(flops, moved, exps=0):
    return pl.CostEstimate(flops=flops // 1000, bytes_accessed=moved // 1000, transcendentals=exps)


def attend_kernel(step, len_ref, q_ref, k_ref, v_ref, o_ref, lse_ref):
    depth = k_ref.shape[-1]
    q = q_ref[0] * (depth**-0.5)
    s = dot_t(k_ref[0], q.astype(BF))
    ids = lax.broadcasted_iota(jnp.int32, s.shape, 0)
    s = jnp.where(ids < len_ref[step], s, MASKED)
    top = jnp.max(s, axis=0, keepdims=True)
    e = jnp.exp(s - top)
    total = jnp.sum(e, axis=0, keepdims=True)
    p = (e * (1.0 / total)).astype(BF)
    o_ref[0] = dot_w(p, v_ref[0]).astype(BF)
    lse_ref[0, 0] = top + jnp.log(total)


def attend(step, qkv, lens, heads, before=(), gate=()):
    micro, rows, all_width = qkv.shape
    depth = all_width // (heads + 2)
    spec = lambda f: pl.BlockSpec((1, rows, depth), f)

    def kernel(*refs):
        attend_kernel(step, *refs)

    return pl.pallas_call(
        chained(kernel, 4, len(before) + len(gate)),
        grid_spec=pltpu.PrefetchScalarGridSpec(
            num_scalar_prefetch=1,
            grid=(heads,),
            in_specs=[
                spec(lambda h, s: (step, 0, h)),
                spec(lambda h, s: (step, 0, heads)),
                spec(lambda h, s: (step, 0, heads + 1)),
            ]
            + kept(len(before) + len(gate)),
            out_specs=[
                spec(lambda h, s: (step, 0, h)),
                pl.BlockSpec((1, 1, 1, rows), lambda h, s: (step, h, 0, 0)),
            ],
        ),
        out_shape=[
            jax.ShapeDtypeStruct((micro, rows, heads * depth), BF),
            jax.ShapeDtypeStruct((micro, heads, 1, rows), F32),
        ],
        input_output_aliases={4 + i: i for i in range(len(before))},
        compiler_params=params(48, 1),
        cost_estimate=cost(4 * heads * rows * rows * depth, 2 * rows * all_width * 2),
        name="attend",
    )(lens, qkv, qkv, qkv, *before, *gate)


def attend_back_kernel(step, len_ref, q_ref, k_ref, v_ref, do_ref, lse_ref, dq_ref, dk_ref, dv_ref):
    depth = k_ref.shape[-1]
    scale = depth**-0.5

    @pl.when(pl.program_id(0) == 0)
    def _():
        dk_ref[...] = jnp.zeros_like(dk_ref)
        dv_ref[...] = jnp.zeros_like(dv_ref)

    q = (q_ref[0] * scale).astype(BF)
    do = do_ref[0]
    s = dot_t(k_ref[0], q)
    ids = lax.broadcasted_iota(jnp.int32, s.shape, 0)
    p = jnp.where(ids < len_ref[step], jnp.exp(s - lse_ref[0, 0]), 0.0)
    dv_ref[0] += dot(p.astype(BF), do)
    dp = dot_t(v_ref[0], do)
    centre = jnp.sum(p * dp, axis=0, keepdims=True)
    ds = (p * (dp - centre)).astype(BF)
    dk_ref[0] += dot(ds, q)
    dq_ref[0] = (dot_w(ds, k_ref[0]) * scale).astype(BF)


def attend_back(step, qkv, dout, lse, lens, heads, before=(), gate=()):
    micro, rows, all_width = qkv.shape
    depth = all_width // (heads + 2)
    spec = lambda f: pl.BlockSpec((1, rows, depth), f)

    def kernel(*refs):
        attend_back_kernel(step, *refs)

    return pl.pallas_call(
        chained(kernel, 6, len(before) + len(gate)),
        grid_spec=pltpu.PrefetchScalarGridSpec(
            num_scalar_prefetch=1,
            grid=(heads,),
            in_specs=[
                spec(lambda h, s: (step, 0, h)),
                spec(lambda h, s: (step, 0, heads)),
                spec(lambda h, s: (step, 0, heads + 1)),
                spec(lambda h, s: (step, 0, h)),
                pl.BlockSpec((1, 1, 1, rows), lambda h, s: (step, h, 0, 0)),
            ]
            + kept(len(before) + len(gate)),
            out_specs=[
                spec(lambda h, s: (step, 0, h)),
                spec(lambda h, s: (step, 0, 0)),
                spec(lambda h, s: (step, 0, 0)),
            ],
        ),
        out_shape=[
            jax.ShapeDtypeStruct((micro, rows, heads * depth), BF),
            jax.ShapeDtypeStruct((micro, rows, depth), F32),
            jax.ShapeDtypeStruct((micro, rows, depth), F32),
        ],
        input_output_aliases={6 + i: i for i in range(len(before))},
        compiler_params=params(48, 1),
        cost_estimate=cost(10 * heads * rows * rows * depth, 5 * rows * all_width * 2),
        name="attend_back",
    )(lens, qkv, qkv, qkv, dout, lse, *before, *gate)


def feed_kernel(
    o_ref, x_ref, cot_ref, wm_ref, gain_ref, wg_ref, wu_ref, wd_ref,
    out_ref, dx_ref, dmixed_ref, dattn_ref, hs_ref, mid_ref, dgate_ref, dup_ref,
    h_ref, acc_ref, dh_ref,
):
    at = pl.program_id(0)
    last = pl.num_programs(0) - 1

    @pl.when(at == 0)
    def _():
        x1 = x_ref[...].astype(F32) + dot(o_ref[...], wm_ref[...])
        h = (normed(x1)[0] * gain_ref[...]).astype(BF)
        h_ref[...] = h
        hs_ref[...] = h
        acc_ref[...] = x1
        dx_ref[...] = x1
        dh_ref[...] = jnp.zeros_like(dh_ref)

    h = h_ref[...]
    dy = cot_ref[...]
    gate = dot(h, wg_ref[...])
    up = dot(h, wu_ref[...])
    dmid = dot_t(dy, wd_ref[...])
    act, slope = gelu_parts(gate)
    mid = (act * up).astype(BF)
    dgate = (dmid * up * slope).astype(BF)
    dup = (dmid * act).astype(BF)
    mid_ref[...] = mid
    dgate_ref[...] = dgate
    dup_ref[...] = dup
    acc_ref[...] += dot(mid, wd_ref[...])
    dh_ref[...] += dot_t(dgate, wg_ref[...]) + dot_t(dup, wu_ref[...])

    @pl.when(at == last)
    def _():
        out_ref[...] = acc_ref[...].astype(BF)
        normal, factor = normed(dx_ref[...])
        dh = dh_ref[...]
        dx = cot_ref[...].astype(F32) + norm_back(dh, normal, factor, gain_ref[...])
        dx_ref[...] = dx
        dmixed = dx.astype(BF)
        dmixed_ref[...] = dmixed
        dattn_ref[...] = dot_t(dmixed, wm_ref[...]).astype(BF)


def feed(step, micro, o, x, cot, wm, gain, wgu, wd, before=(), gate=()):
    total, width = x.shape
    rows = total // micro
    hq, ff = o.shape[1], wd.shape[0]
    unit = 512
    chunks = ff // unit
    once = dict(pipeline_mode=pl.Buffered(1))
    row = lambda w: pl.BlockSpec((rows, w), lambda i: (step, 0), **once)
    col = lambda f: pl.BlockSpec((rows, unit), f)
    whole = lambda a: pl.BlockSpec(a.shape, lambda i: (0, 0), **once)
    out = lambda w, t: jax.ShapeDtypeStruct((total, w), t)
    kernel = chained(feed_kernel, 8, len(before) + len(gate))
    return pl.pallas_call(
        kernel,
        grid=(chunks,),
        in_specs=[row(hq), row(width), row(width), whole(wm), whole(gain)]
        + [
            pl.BlockSpec((width, unit), lambda i: (0, i)),
            pl.BlockSpec((width, unit), lambda i: (0, chunks + i)),
            pl.BlockSpec((unit, width), lambda i: (i, 0)),
        ]
        + kept(len(before) + len(gate)),
        out_specs=[row(width), row(width), row(width), row(hq), row(width)]
        + [col(lambda i: (step, i))] * 3,
        out_shape=[
            out(width, BF), out(width, F32), out(width, BF), out(hq, BF), out(width, BF),
            out(ff, BF), out(ff, BF), out(ff, BF),
        ],
        scratch_shapes=[
            pltpu.VMEM((rows, width), BF),
            pltpu.VMEM((rows, width), F32),
            pltpu.VMEM((rows, width), F32),
        ],
        input_output_aliases={8 + i: i for i in range(len(before))},
        compiler_params=params(60, 1),
        cost_estimate=cost(rows * (12 * width * ff + 4 * width * hq), rows * ff * 8 + wgu.size * 3),
        name="feed",
    )(o, x, cot, wm, gain, wgu, wgu, wd, *before, *gate)


def weight_grad_kernel(spread, x_ref, *refs):
    if spread:
        spread_ref, *refs = refs
    *g_refs, out_ref, turned_ref = refs
    at = pl.program_id(0)

    @pl.when(at == 0)
    def _():
        if spread:
            turned_ref[...] = lax.dot_general(
                spread_ref[...],
                x_ref[...],
                (((0,), (1,)), ((), ())),
                preferred_element_type=F32,
            ).astype(BF)
        else:
            turned_ref[...] = x_ref[...].T

    each = pl.num_programs(0) // len(g_refs)
    for i, g_ref in enumerate(g_refs):

        @pl.when(at // each == i)
        def _():
            out_ref[...] = dot(turned_ref[...], g_ref[...]).astype(BF)


def weight_grad(x, grads, unit, spread=None, gate=()):
    rows, width = x.shape
    each = grads[0].shape[1] // unit
    count = each * len(grads)
    columns = count * unit
    whole = lambda a: pl.BlockSpec(a.shape, lambda at: (0, 0), pipeline_mode=pl.Buffered(1))
    extra = [] if spread is None else [spread]
    width = width if spread is None else spread.shape[1]

    def kernel(*refs):
        weight_grad_kernel(spread is not None, *refs)

    def place(i):
        return pl.BlockSpec(
            (rows, unit), lambda at: (0, jnp.clip(at - i * each, 0, each - 1))
        )

    return pl.pallas_call(
        chained(kernel, 1 + len(extra) + len(grads), len(gate)),
        grid=(count,),
        in_specs=[whole(a) for a in [x] + extra]
        + [place(i) for i in range(len(grads))]
        + kept(len(gate)),
        out_specs=pl.BlockSpec((width, unit), lambda at: (0, at)),
        out_shape=jax.ShapeDtypeStruct((width, columns), BF),
        scratch_shapes=[pltpu.VMEM((width, rows), BF)],
        compiler_params=params(48, 1),
        cost_estimate=cost(2 * rows * width * count * unit, 2 * rows * (width + count * unit)),
        name="weight_grad",
    )(x, *extra, *grads, *gate)


def stack_heads(x, heads):
    depth = x.shape[-1] // heads
    return jnp.concatenate([x[:, h * depth : (h + 1) * depth] for h in range(heads)], axis=0)


def own_scores(heads, scale, length, seg_len, qkv_ref, k_ref):
    depth = k_ref.shape[-1]
    qkv = qkv_ref[0, 0].astype(F32)
    q = (stack_heads(qkv[:, : heads * depth], heads) * scale).astype(BF)
    near_k = qkv[:, heads * depth : (heads + 1) * depth].astype(BF)
    near_v = qkv[:, (heads + 1) * depth :].astype(BF)
    far = dot_t(k_ref[0], q)
    near = dot_t(near_k, q)
    far_ok = lax.broadcasted_iota(jnp.int32, far.shape, 0) < length
    near_ok = lax.broadcasted_iota(jnp.int32, near.shape, 0) < seg_len
    return q, near_k, near_v, jnp.where(far_ok, far, MASKED), jnp.where(near_ok, near, MASKED)


def own_kernel(heads, seg_len, own_ref, len_ref, qkv_ref, k_ref, v_ref, o_ref, lse_ref):
    m, c = pl.program_id(0), pl.program_id(1)
    mine = own_ref[m * pl.num_programs(1) + c] == 1
    depth = k_ref.shape[-1]
    rows = qkv_ref.shape[2]

    @pl.when(mine)
    def _():
        q, near_k, near_v, far, near = own_scores(
            heads, depth**-0.5, len_ref[m], seg_len, qkv_ref, k_ref
        )
        top = jnp.maximum(
            jnp.max(far, axis=0, keepdims=True), jnp.max(near, axis=0, keepdims=True)
        )
        far, near = jnp.exp(far - top), jnp.exp(near - top)
        total = jnp.sum(far, axis=0, keepdims=True) + jnp.sum(near, axis=0, keepdims=True)
        part = 1.0 / total
        o = dot_w((far * part).astype(BF), v_ref[0]) + dot_w((near * part).astype(BF), near_v)
        for h in range(heads):
            o_ref[0, 0, :, h * depth : (h + 1) * depth] = o[h * rows : (h + 1) * rows].astype(BF)
        lse_ref[0, 0] = top + jnp.log(total)

    @pl.when(jnp.logical_not(mine))
    def _():
        o_ref[...] = jnp.zeros_like(o_ref)
        lse_ref[...] = jnp.zeros_like(lse_ref)


def own_attend(seg_qkv, qkv, own, lens, heads, seg_len):
    n, micro, rows, all_width = seg_qkv.shape
    depth = all_width // (heads + 2)
    prefix = qkv.shape[1]
    seg = lambda w: pl.BlockSpec((1, 1, rows, w), lambda m, c, a, b: (c, m, 0, 0))
    stat = pl.BlockSpec((1, 1, 1, heads * rows), lambda m, c, a, b: (c, m, 0, 0))

    def kernel(*refs):
        own_kernel(heads, seg_len, *refs)

    return pl.pallas_call(
        kernel,
        grid_spec=pltpu.PrefetchScalarGridSpec(
            num_scalar_prefetch=2,
            grid=(micro, n),
            in_specs=[
                seg(all_width),
                pl.BlockSpec((1, prefix, depth), lambda m, c, a, b: (m, 0, heads)),
                pl.BlockSpec((1, prefix, depth), lambda m, c, a, b: (m, 0, heads + 1)),
            ],
            out_specs=[seg(heads * depth), stat],
        ),
        out_shape=[
            jax.ShapeDtypeStruct((n, micro, rows, heads * depth), BF),
            jax.ShapeDtypeStruct((n, micro, 1, heads * rows), F32),
        ],
        compiler_params=params(32, 2),
        cost_estimate=cost(4 * 2 * micro * heads * rows * prefix * depth, 4 * seg_qkv.size),
        name="own_attend",
    )(own, lens, seg_qkv, qkv, qkv)


def own_back_kernel(
    heads, seg_len, own_ref, len_ref, qkv_ref, k_ref, v_ref, do_ref, lse_ref, dqkv_ref, dk_ref, dv_ref
):
    m, c = pl.program_id(0), pl.program_id(1)
    mine = own_ref[m * pl.num_programs(1) + c] == 1
    depth = k_ref.shape[-1]
    rows = qkv_ref.shape[2]
    scale = depth**-0.5

    @pl.when(c == 0)
    def _():
        dk_ref[...] = jnp.zeros_like(dk_ref)
        dv_ref[...] = jnp.zeros_like(dv_ref)

    @pl.when(mine)
    def _():
        q, near_k, near_v, far, near = own_scores(heads, scale, len_ref[m], seg_len, qkv_ref, k_ref)
        far, near = jnp.exp(far - lse_ref[0, 0]), jnp.exp(near - lse_ref[0, 0])
        do = stack_heads(do_ref[0, 0].astype(F32), heads).astype(BF)
        dv_ref[0] += dot(far.astype(BF), do)
        dfar, dnear = dot_t(v_ref[0], do), dot_t(near_v, do)
        centre = jnp.sum(far * dfar, axis=0, keepdims=True)
        centre = centre + jnp.sum(near * dnear, axis=0, keepdims=True)
        sfar = (far * (dfar - centre)).astype(BF)
        snear = (near * (dnear - centre)).astype(BF)
        dk_ref[0] += dot(sfar, q)
        dq = (dot_w(sfar, k_ref[0]) + dot_w(snear, near_k)) * scale
        for h in range(heads):
            dqkv_ref[0, 0, :, h * depth : (h + 1) * depth] = dq[h * rows : (h + 1) * rows].astype(BF)
        dqkv_ref[0, 0, :, heads * depth : (heads + 1) * depth] = dot(snear, q).astype(BF)
        dqkv_ref[0, 0, :, (heads + 1) * depth :] = dot(near.astype(BF), do).astype(BF)

    @pl.when(jnp.logical_not(mine))
    def _():
        dqkv_ref[...] = jnp.zeros_like(dqkv_ref)


def own_back(seg_qkv, qkv, dout, lse, own, lens, heads, seg_len):
    n, micro, rows, all_width = seg_qkv.shape
    depth = all_width // (heads + 2)
    prefix = qkv.shape[1]
    seg = lambda w: pl.BlockSpec((1, 1, rows, w), lambda m, c, a, b: (c, m, 0, 0))
    item = lambda i: pl.BlockSpec((1, prefix, depth), lambda m, c, a, b: (m, 0, i))

    def kernel(*refs):
        own_back_kernel(heads, seg_len, *refs)

    return pl.pallas_call(
        kernel,
        grid_spec=pltpu.PrefetchScalarGridSpec(
            num_scalar_prefetch=2,
            grid=(micro, n),
            in_specs=[
                seg(all_width),
                item(heads),
                item(heads + 1),
                seg(heads * depth),
                pl.BlockSpec((1, 1, 1, heads * rows), lambda m, c, a, b: (c, m, 0, 0)),
            ],
            out_specs=[seg(all_width), item(0), item(0)],
        ),
        out_shape=[
            jax.ShapeDtypeStruct((n, micro, rows, all_width), BF),
            jax.ShapeDtypeStruct((micro, prefix, depth), F32),
            jax.ShapeDtypeStruct((micro, prefix, depth), F32),
        ],
        compiler_params=params(32, 2),
        cost_estimate=cost(10 * 2 * micro * heads * rows * prefix * depth, 8 * seg_qkv.size),
        name="own_back",
    )(own, lens, seg_qkv, qkv, qkv, dout, lse)


def per_device(
    prefix_rows,
    action_rows,
    segment_item,
    segment_time,
    item_weight,
    prefix_len,
    vlm_prenorm,
    vlm_query,
    vlm_key,
    vlm_value,
    vlm_mixer,
    vlm_midnorm,
    vlm_gate,
    vlm_expand,
    vlm_down,
    act_prenorm,
    act_query,
    act_key,
    act_value,
    act_mixer,
    act_midnorm,
    act_gate,
    act_expand,
    act_down,
    time_scales,
    cot_prefix,
    cot_action,
):
    micro, items, prefix, width = prefix_rows.shape
    seg_len, wide = action_rows.shape[2:]
    groups, n = lax.axis_size("dp"), lax.axis_size("noise")
    depth, hq = vlm_key.shape[1], vlm_query.shape[1]
    heads = hq // depth
    width_qkv = hq + 2 * depth
    ff, ffa = vlm_gate.shape[1], act_gate.shape[1]
    levels = time_scales.shape[1]
    rows_p, rows_a = vlm_query.shape[0], act_query.shape[0]
    here = lax.axis_index("noise")
    every, line = Line(ALL), Line("noise")
    total = every.count
    dp = Line("dp")
    slot = -(-(seg_len + 1) // 8) * 8
    block = micro * slot

    lanes = lambda x, w: jnp.pad(x, ((0, 0), (0, w - x.shape[1])))
    gap = -(-rows_p // 8) * 8
    taller = lambda x: jnp.pad(x, ((0, gap - rows_p), (0, 0)))
    rows_m = vlm_mixer.shape[0]
    unit = act_down.shape[0]
    part = groups * unit

    item, time = segment_item[:, 0], segment_time[:, 0]
    spare = jnp.zeros((micro, slot - seg_len, wide), BF)
    tags = spare.at[:, 0, 0].set(item.astype(BF)).at[:, 0, 1].set(time.astype(BF))
    action_in = jnp.concatenate([action_rows[:, 0], tags], axis=1)
    hot = item[:, None] == jnp.arange(prefix_len.shape[1])[None, :]
    weight = (jnp.sum(jnp.where(hot, item_weight, 0), axis=1) + 1).astype(F32) / 8.0
    grad_action = cot_action[:, 0].astype(F32) * weight[:, None, None]
    grad_action = jnp.pad(grad_action, ((0, 0), (0, slot - seg_len), (0, 0)))

    pre_pack = jnp.concatenate(
        [
            vlm_query,
            vlm_key,
            vlm_value,
            lanes(jnp.stack([vlm_prenorm, vlm_midnorm], axis=1), 128),
        ],
        axis=1,
    )
    act_small = [act_prenorm[:, None], act_midnorm[:, None], time_scales.reshape(rows_a, -1)]
    act_pack = [act_query, act_key, act_value, lanes(jnp.concatenate(act_small, axis=1), 128)]
    act_pack = jnp.concatenate(act_pack, axis=1)
    fold = jnp.concatenate([vlm_mixer, vlm_down], axis=0)
    second = [taller(vlm_gate), taller(vlm_expand), tiles(fold, gap), tiles(act_mixer, gap)]
    cut = 2 * ff + second[2].shape[1]
    second = lax.all_gather(jnp.concatenate(second, axis=1), ALL, axis=0)

    def beside(near):
        cols = jnp.stack([act_gate, act_expand]).reshape(2, rows_a, groups, n, unit)
        cols = cols.transpose(3, 0, 1, 2, 4).reshape(n, 2, rows_a, part)
        (cols,) = after([cols], near)
        return lax.all_to_all(cols, "noise", 0, 0, tiled=True)

    first = jnp.concatenate([act_pack, taller(pre_pack)], axis=0)
    first, seg_all, cols = fetch(first, action_in, dp, line, beside)
    cols = cols.transpose(0, 2, 1, 3).reshape(n * rows_a, 2 * part)
    hidden_w = jnp.concatenate([cols, act_down.reshape(-1, 2 * part)], axis=0)
    dy_own = grad_action.astype(BF).reshape(block, wide)
    act_a = first[:, :rows_a].reshape(total * rows_a, -1)
    pre_a = first[:, rows_a:].reshape(total * gap, -1)

    places = jnp.arange(total * gap)
    spread = (places // gap * rows_p + places % gap)[None, :] == jnp.arange(width)[:, None]
    spread = (spread & (places % gap < rows_p)[None, :]).astype(BF)
    pre_a = dot(spread, pre_a).astype(BF)
    pre_qkv = pre_a[:, :width_qkv]
    pre_gain = pre_a[:, width_qkv].astype(F32)
    pre_midgain = pre_a[:, width_qkv + 1].astype(F32)
    suf_qkv = act_a[:, :width_qkv]
    small = act_a[:, width_qkv:].astype(F32)
    suf_gain, suf_midgain = small[:, 0], small[:, 1]
    table = small[:, 2 : 2 + time_scales.size // rows_a].reshape(2 * wide, levels)

    times = seg_all[:, :, seg_len, 1].astype(jnp.int32)
    own = (seg_all[:, :, seg_len, 0].astype(jnp.int32) == here).astype(jnp.int32)
    own = own.T.reshape(-1)
    is_row = (jnp.arange(slot) < seg_len)[:, None]
    hots = (times[..., None] == jnp.arange(levels)).astype(F32)
    mods = jnp.einsum("nmt,jt->nmj", hots, table, precision=HIGH)
    mod1_all = mods[:, :, None, :wide]
    mod2 = mods[0, :, None, wide:]
    an1, as1 = normed(jnp.where(is_row, seg_all, 0).astype(F32))
    ah1 = flatten((an1 * suf_gain * mod1_all).astype(BF))
    seg_qkv = dot(ah1, suf_qkv).astype(BF).reshape(n, micro, slot, width_qkv)

    x = prefix_rows[:, 0]
    n1, s1 = normed(x.astype(F32))
    h1 = flatten((n1 * pre_gain).astype(BF))
    qkv = dot(h1, pre_qkv).astype(BF).reshape(micro, prefix, width_qkv)
    lens = lax.dynamic_slice_in_dim(prefix_len, here, 1, axis=1)[:, 0]

    oa, lse_a = own_attend(seg_qkv, qkv, own, lens, heads, seg_len)

    oa = line.home(oa.reshape(n, block, hq))
    hidden_w, dy_own = after([hidden_w, dy_own], oa)
    hidden_w = jnp.stack([hidden_w] + [dp.across(hidden_w, k) for k in range(1, groups)])
    hidden_w = turned(hidden_w, dp.me)
    dy_all = line.around(dy_own).reshape(-1, wide)
    gu_w = hidden_w[:, : n * rows_a].reshape(-1, 2 * part)
    down_w = hidden_w[:, n * rows_a :].reshape(part, wide)
    outs = attend(0, qkv, lens, heads, (), (seg_qkv,))
    outs = attend(1, qkv, lens, heads, outs, (oa,))
    o, lse = outs
    oa = line.home_end(oa, (o,)).astype(BF)
    suf_mixer = tiles(second[..., cut:], gap, act_mixer.shape)
    a1 = jnp.where(is_row, action_in, 0).astype(F32) + dot(oa, suf_mixer).reshape(micro, slot, wide)
    an2, as2 = normed(a1)
    ah2 = (an2 * suf_midgain * mod2).astype(BF).reshape(block, wide)

    h_all = line.around(ah2).reshape(n * block, wide)
    gu = dot(h_all, gu_w)
    gate_a, up_a = gu[:, :part], gu[:, part:]
    act_g, slope_g = gelu_parts(gate_a)
    mid_a = (act_g * up_a).astype(BF)
    dmid_a = dot_t(dy_all, down_w)
    dgu = jnp.concatenate(
        [(dmid_a * up_a * slope_g).astype(BF), (dmid_a * act_g).astype(BF)], axis=1
    )
    grad_late = line.home(dot_t(dgu, gu_w).astype(BF).reshape(n, block, wide))
    out_a = turned(dot(mid_a, down_w).astype(BF).reshape(n, block, wide), here)
    out_a = lax.psum_scatter(out_a, "noise", scatter_dimension=0)
    dff = jnp.concatenate(
        [
            dot_w(h_all, dgu).astype(BF).reshape(groups, n * rows_a, 2 * part),
            dot_w(mid_a, dy_all).astype(BF).reshape(groups, -1, 2 * part),
        ],
        axis=1,
    )
    dff = dff.reshape(-1, 2 * part)
    dff = lax.psum_scatter(dff, "dp", scatter_dimension=0, tiled=True)

    pre_gu = dot(spread, second[..., : 2 * ff].reshape(total * gap, -1)).astype(BF)
    fold = tiles(second[..., 2 * ff : cut], gap, fold.shape).reshape(total, -1, width)
    pre_mixer = fold[:, :rows_m].reshape(hq, width)
    pre_down = fold[:, rows_m:].reshape(ff, width)
    cot = cot_prefix.reshape(micro * prefix, width)

    def feed_half(step, outs, gate):
        return feed(
            step, micro, o.reshape(-1, hq), x.reshape(-1, width), cot,
            pre_mixer, pre_midgain[None], pre_gu, pre_down, outs, gate,
        )

    outs = feed_half(0, (), (grad_late,))
    grad_late = line.home_end(grad_late, (outs[0],)).reshape(micro, slot, wide)
    late_back = grad_late * an2
    dmod2 = jnp.sum(late_back * suf_midgain, axis=1)
    da1 = grad_action + norm_back(grad_late, an2, as2, suf_midgain * mod2)
    dmixed_a = da1.astype(BF).reshape(block, wide)
    dattn_a = dot_t(dmixed_a, suf_mixer).astype(BF)
    outs = feed_half(1, outs, (dattn_a,))
    prefix_out, dx1, dmixed, dattn, h2, mid, dgate, dup = outs
    dattn_all = line.around(dattn_a, (dx1,)).reshape(n, micro, slot, hq)

    big_w = weight_grad(h2, [dgate, dup], 512, spread)
    big_sum = Sum(big_w.reshape(total, gap, -1), dp, line)
    big_way = joint(big_sum.cores())

    (dattn_all,) = after([dattn_all], big_w)
    dseg, far_dk, far_dv = own_back(seg_qkv, qkv, dattn_all, lse_a, own, lens, heads, seg_len)
    dseg = dseg.reshape(n * block, width_qkv)
    dah1 = dot_t(dseg, suf_qkv).reshape(n, micro, slot, wide)
    dmod1 = jnp.sum(dah1 * an1 * suf_gain, axis=2)
    back = norm_back(dah1, an1, as1, suf_gain * mod1_all).astype(BF).reshape(n, block, wide)
    dtable = jnp.concatenate(
        [
            jnp.einsum("nmj,nmt->jt", dmod1, hots, precision=HIGH),
            jnp.einsum("mj,mt->jt", dmod2, hots[0], precision=HIGH),
        ],
        axis=0,
    )
    table_cols = dtable.size // wide
    dtable = lanes(dtable.reshape(wide, table_cols), 128).astype(BF)
    act_w = jnp.concatenate([dot_w(ah1, dseg).astype(BF), dtable], axis=1)
    act_sum = Sum(act_w.reshape(total, rows_a, -1), dp, line)
    big_sum.take(big_way)

    early = (big_sum.x, act_w)
    dmd_w = jnp.concatenate(
        [
            weight_grad(o.reshape(-1, hq), [dmixed], width, gate=early).reshape(
                total, rows_m, width
            ),
            weight_grad(mid, [cot], width, gate=early).reshape(total, -1, width),
        ],
        axis=1,
    )
    grads = [dmd_w, dot_w(oa, dmixed_a).astype(BF).reshape(total, rows_a, -1)]
    grads = [jax.vmap(lambda g: tiles(g, gap))(g) for g in grads]
    cut = grads[0].shape[-1]
    grads = jnp.concatenate(grads, axis=-1)
    grads_sum = lax.psum_scatter(grads, ALL, scatter_dimension=0)
    dmd_w = tiles(grads_sum[:, :cut], gap, dmd_w.shape[1:])
    dam_w = tiles(grads_sum[:, cut:], gap, (rows_a, wide))

    dattn = dattn.reshape(micro, prefix, hq)
    outs = attend_back(0, qkv, dattn, lse, lens, heads, (), (grads,))
    *big_way, act_way = joint(big_sum.groups() + act_sum.cores(), outs[0])
    big_sum.take(big_way)
    act_sum.take([act_way])
    outs = attend_back(1, qkv, dattn, lse, lens, heads, outs, (big_sum.x, act_sum.x))
    dq, dk, dv = outs
    big_way, *act_way = joint(big_sum.along() + act_sum.groups(), dq)
    big_sum.take([big_way])
    act_sum.take(act_way)
    dkv = jnp.concatenate([(dk + far_dk).astype(BF), (dv + far_dv).astype(BF)], axis=-1)
    dqkv = jnp.concatenate([dq, dkv], axis=-1).reshape(-1, width_qkv)
    pre_w = weight_grad(h1, [dqkv], 512, spread, (big_sum.x, act_sum.x))
    back = back.reshape((n // 2, 2) + back.shape[1:])
    jobs = [big_sum.along() if big_sum.bits else [], act_sum.along(), [(line, back[:, 1], 1)]]
    *ways, back_way = joint(sum(jobs, []), pre_w)
    for way, each in zip(ways, [s for s, j in zip((big_sum, act_sum), jobs) if j]):
        each.take([way])
    back = back[:, 0] + back_way
    pre_sum = Sum(pre_w.reshape(total, gap, -1), dp, line)
    jobs = act_sum.along() if act_sum.bits else []
    *ways, pre_way = joint(jobs + pre_sum.cores(), back)
    for way in ways:
        act_sum.take([way])
    pre_sum.take([pre_way])
    pre_sum.take(joint(pre_sum.groups()))
    (dqkv, back) = after([dqkv, back], pre_w)

    (dff,) = after([dff], pre_w)
    ddown_a = dff[n * rows_a :].reshape(unit, wide)
    dgu_a = dff[: n * rows_a].reshape(n, rows_a, 2 * part)
    dgu_a = lax.all_to_all(dgu_a, "noise", 0, 0, tiled=True)
    dgu_a = dgu_a.reshape(n, rows_a, 2, groups, unit).transpose(2, 1, 3, 0, 4)
    dgu_a = dgu_a.reshape(2, rows_a, ffa).astype(F32)
    back = line.home_end(back).reshape(micro, slot, wide)
    action_out = (a1 + out_a.reshape(micro, slot, wide))[:, :seg_len].astype(BF)
    action_grad = (da1 + back)[:, :seg_len]
    dh1 = dot_t(dqkv, pre_qkv).reshape(micro, prefix, width)
    prefix_grad = dx1.reshape(micro, prefix, width) + norm_back(dh1, n1, s1, pre_gain)

    big_g = big_sum.result()[:rows_p]
    act_g = act_sum.result()
    pre_g = pre_sum.result()[:rows_p]

    def gain_grad(pairs, gain):
        sums = sum(jnp.sum(w.astype(F32) * dw, axis=1) for w, dw in pairs)
        return sums / gain.astype(F32)

    pre_pairs = [
        (vlm_query, pre_g[:, :hq]),
        (vlm_key, pre_g[:, hq : hq + depth]),
        (vlm_value, pre_g[:, hq + depth :]),
    ]
    mid_pairs = [(vlm_gate, big_g[:, :ff]), (vlm_expand, big_g[:, ff:])]
    act_pairs = [
        (act_query, act_g[:, :hq]),
        (act_key, act_g[:, hq : hq + depth]),
        (act_value, act_g[:, hq + depth : width_qkv]),
    ]
    late_pairs = [(act_gate, dgu_a[0]), (act_expand, dgu_a[1])]
    return (
        prefix_out.reshape(prefix_rows.shape),
        action_out[:, None],
        prefix_grad[:, None],
        action_grad[:, None],
        gain_grad(pre_pairs, vlm_prenorm),
        pre_g[:, :hq],
        pre_g[:, hq : hq + depth],
        pre_g[:, hq + depth :],
        dmd_w[:rows_m].astype(F32),
        gain_grad(mid_pairs, vlm_midnorm),
        big_g[:, :ff],
        big_g[:, ff:],
        dmd_w[rows_m:].astype(F32),
        gain_grad(act_pairs, act_prenorm),
        act_g[:, :hq],
        act_g[:, hq : hq + depth],
        act_g[:, hq + depth : width_qkv],
        dam_w.astype(F32),
        gain_grad(late_pairs, act_midnorm),
        dgu_a[0],
        dgu_a[1],
        ddown_a.astype(F32),
        act_g[:, width_qkv : width_qkv + table_cols].reshape(-1, levels),
    )


def solution(mesh):
    return jax.shard_map(
        per_device,
        mesh=mesh,
        in_specs=(
            P(None, ("dp", "noise"), None, None),
            P(None, ("dp", "noise"), None, None),
            P(None, ("dp", "noise")),
            P(None, ("dp", "noise")),
            P(None, "dp"),
            P(None, "dp"),
            P(("dp", "noise")),
            P(("dp", "noise"), None),
            P(("dp", "noise"), None),
            P(("dp", "noise"), None),
            P(("dp", "noise"), None),
            P(("dp", "noise")),
            P(("dp", "noise"), None),
            P(("dp", "noise"), None),
            P(("dp", "noise"), None),
            P(("dp", "noise")),
            P(("dp", "noise"), None),
            P(("dp", "noise"), None),
            P(("dp", "noise"), None),
            P(("dp", "noise"), None),
            P(("dp", "noise")),
            P(("dp", "noise"), None),
            P(("dp", "noise"), None),
            P(("dp", "noise"), None),
            P(("dp", "noise"), None),
            P(None, ("dp", "noise"), None, None),
            P(None, ("dp", "noise"), None, None),
        ),
        out_specs=(
            P(None, ("dp", "noise"), None, None),
            P(None, ("dp", "noise"), None, None),
            P(None, ("dp", "noise"), None, None),
            P(None, ("dp", "noise"), None, None),
            P(("dp", "noise")),
            P(("dp", "noise"), None),
            P(("dp", "noise"), None),
            P(("dp", "noise"), None),
            P(("dp", "noise"), None),
            P(("dp", "noise")),
            P(("dp", "noise"), None),
            P(("dp", "noise"), None),
            P(("dp", "noise"), None),
            P(("dp", "noise")),
            P(("dp", "noise"), None),
            P(("dp", "noise"), None),
            P(("dp", "noise"), None),
            P(("dp", "noise"), None),
            P(("dp", "noise")),
            P(("dp", "noise"), None),
            P(("dp", "noise"), None),
            P(("dp", "noise"), None),
            P(("dp", "noise"), None),
        ),
        check_vma=False,
    )
```

```python
import jax
import jax.numpy as jnp
from jax import lax
from jax.experimental import pallas as pl
from jax.experimental.pallas import tpu as pltpu
from jax.sharding import PartitionSpec as P

EPS = 1e-06
HIGH = lax.Precision.HIGHEST
ALL = ("dp", "noise")
BF = jnp.bfloat16
F32 = jnp.float32
ROOT = 0.7978845608028654
MASKED = -1e30


def normed(rows):
    factor = lax.rsqrt(jnp.mean(rows * rows, axis=-1, keepdims=True) + EPS)
    return (rows * factor, factor)


def norm_back(grad_hidden, normal, factor, gain_mod):
    grad_normal = grad_hidden * gain_mod
    centred = jnp.mean(grad_normal * normal, axis=-1, keepdims=True)
    return factor * (grad_normal - normal * centred)


def flatten(array):
    return array.reshape(-1, array.shape[-1])


def gelu_parts(gate):
    square = gate * gate
    t = jnp.tanh(gate * (ROOT + (ROOT * 0.044715) * square))
    half = 0.5 + 0.5 * t
    slope = half + (gate * (1.0 - t * t)) * ((0.5 * ROOT) + (1.5 * 0.044715 * ROOT) * square)
    return gate * half, slope


def dot(a, b):
    return lax.dot_general(a, b, (((1,), (0,)), ((), ())), preferred_element_type=F32)


def dot_t(a, b):
    return lax.dot_general(a, b, (((1,), (1,)), ((), ())), preferred_element_type=F32)


def dot_w(a, b):
    return lax.dot_general(a, b, (((0,), (0,)), ((), ())), preferred_element_type=F32)


class Line:
    def __init__(self, axes):
        self.axes = axes
        names = (axes,) if isinstance(axes, str) else axes
        self.count, self.me = 1, 0
        for name in names:
            self.count *= lax.axis_size(name)
            self.me = self.me * lax.axis_size(name) + lax.axis_index(name)
        self.bits = list(range(self.count.bit_length() - 1))

    def across(self, x, mask):
        return lax.ppermute(x, self.axes, [(i, i ^ mask) for i in range(self.count)])

    def swap(self, x, bit):
        return self.across(x, 1 << bit)

    def around(self, x, gate=()):
        parts = [self.across(x, far << 1) for far in range(1, self.count // 2)]
        if gate:
            parts = list(after(parts, *gate))
        parts = jnp.stack([x] + parts)
        both = jnp.stack([parts, self.swap(parts, 0)], axis=1)
        return both.reshape((self.count,) + x.shape)

    def home(self, x):
        x = x.reshape((self.count // 2, 2) + x.shape[1:])
        return x[:, 0] + self.swap(x[:, 1], 0)

    def home_end(self, x, gate=()):
        parts = [self.across(x[far], far << 1) for far in range(1, self.count // 2)]
        if gate:
            parts = list(after(parts, *gate))
        return sum((part.astype(F32) for part in parts), x[0].astype(F32))


def joint(jobs, *gate):
    return list(after([line.across(x, mask) for line, x, mask in jobs], *gate))


def fetch(x, rows, dp, line, beside):
    far, count = line.count // 2, dp.count
    *got, more = joint([(line, x, k << 1) for k in range(1, far)] + [(line, rows, 2)])
    near = jnp.stack([x] + got)
    rows = jnp.stack([rows, more])
    jobs = [(dp, near, k) for k in range(1, count)]
    for bit in range(2, far.bit_length()):
        more = line.across(rows, 1 << bit)
        if bit + 1 < far.bit_length():
            rows = jnp.concatenate([rows, more])
    done = beside(near)
    got = [line.across(x, mask) for line, x, mask in jobs]
    *got, more, done = after(got + [more, done])
    same = jnp.stack([near] + got)
    rows = jnp.concatenate([rows, more])
    other, more = joint([(line, same, 1), (line, rows, 1)])
    rows = jnp.stack([rows, more], axis=1).reshape((line.count,) + rows.shape[1:])

    def kernel(me_ref, same_ref, other_ref, out_ref):
        for kd in range(count):
            for kz in range(far):
                at = (me_ref[0] ^ kd) * line.count + (me_ref[1] ^ (2 * kz))
                out_ref[at] = same_ref[kd, kz]
                out_ref[at ^ 1] = other_ref[kd, kz]

    def whole(a):
        return pl.BlockSpec(a, lambda i, me: (0,) * len(a), pipeline_mode=pl.Buffered(1))

    shape = (count * line.count,) + x.shape
    me = jnp.stack([dp.me, line.me]).astype(jnp.int32)
    return pl.pallas_call(
        kernel,
        grid_spec=pltpu.PrefetchScalarGridSpec(
            num_scalar_prefetch=1,
            grid=(1,),
            in_specs=[whole(same.shape)] * 2,
            out_specs=whole(shape),
        ),
        out_shape=jax.ShapeDtypeStruct(shape, x.dtype),
        compiler_params=params(48, 1),
        name="settle",
    )(me, same, other), rows, done


class Sum:
    def __init__(self, x, dp, line):
        self.x, self.dp, self.line = x, dp, line
        self.rest = x.shape[1:]
        self.bits = list(range(1, line.count.bit_length() - 1))

    def half(self, lead, bit, tail):
        x = self.x.reshape(lead + (2,) + tail + self.rest)
        mine = (self.line.me >> bit) & 1
        self.x = lax.dynamic_index_in_dim(x, mine, len(lead), keepdims=False)
        send = lax.dynamic_index_in_dim(x, 1 - mine, len(lead), keepdims=False)
        return [(self.line, send, 1 << bit)]

    def cores(self):
        return self.half((self.dp.count, self.line.count // 2), 0, ())

    def groups(self):
        take = lambda k: lax.dynamic_index_in_dim(self.x, self.dp.me ^ k, 0, keepdims=False)
        jobs = [(self.dp, take(k), k) for k in range(1, self.dp.count)]
        self.x = take(0)
        return jobs

    def along(self):
        far = self.x.shape[0] if self.x.ndim > len(self.rest) else 1
        return self.half((far // 2,), self.bits.pop(0), ())

    def take(self, got):
        kind = self.x.dtype
        self.x = sum((x.astype(F32) for x in got), self.x.astype(F32)).astype(kind)

    def result(self):
        while self.bits:
            self.take([line.across(x, mask) for line, x, mask in self.along()])
        return self.x.reshape(self.rest).astype(F32)


def turned(x, me):
    count = x.shape[0]

    def kernel(me_ref, x_ref, out_ref):
        for k in range(count):
            out_ref[me_ref[0] ^ k] = x_ref[k]

    whole = pl.BlockSpec(x.shape, lambda i, me: (0,) * x.ndim, pipeline_mode=pl.Buffered(1))
    return pl.pallas_call(
        kernel,
        grid_spec=pltpu.PrefetchScalarGridSpec(
            num_scalar_prefetch=1, grid=(1,), in_specs=[whole], out_specs=whole
        ),
        out_shape=jax.ShapeDtypeStruct(x.shape, x.dtype),
        compiler_params=params(32, 1),
        name="turn",
    )(me.astype(jnp.int32)[None], x)


def tiles(x, gap, back=None):
    if back is None:
        rows, cols = x.shape
        count = rows // 8 * (cols // 128)
        high = gap // 8
        wide = -(-count // high)
        x = x.reshape(rows // 8, 8, cols // 128, 128).transpose(0, 2, 1, 3).reshape(count, 8, 128)
        x = jnp.pad(x, ((0, high * wide - count), (0, 0), (0, 0)))
        return x.reshape(high, wide, 8, 128).transpose(0, 2, 1, 3).reshape(gap, wide * 128)
    rows, cols = back
    count = rows // 8 * (cols // 128)
    high, wide = gap // 8, x.shape[-1] // 128
    x = x.reshape(-1, high, 8, wide, 128).transpose(0, 1, 3, 2, 4).reshape(-1, high * wide, 8, 128)
    x = x[:, :count].reshape(-1, rows // 8, cols // 128, 8, 128).transpose(0, 1, 3, 2, 4)
    return x.reshape(-1, cols)


def params(megabytes, dims):
    return pltpu.CompilerParams(
        vmem_limit_bytes=megabytes << 20, dimension_semantics=("arbitrary",) * dims
    )


def chained(kernel, at, count):
    def inner(*refs):
        kernel(*refs[:at], *refs[at + count :])

    return inner


def kept(count):
    return [pl.BlockSpec(memory_space=pl.ANY)] * count


def after(values, *others):
    def kernel(*refs):
        pass

    where = pl.BlockSpec(memory_space=pl.ANY)
    return pl.pallas_call(
        kernel,
        in_specs=[where] * (len(values) + len(others)),
        out_specs=[where] * len(values),
        out_shape=[jax.ShapeDtypeStruct(v.shape, v.dtype) for v in values],
        input_output_aliases={i: i for i in range(len(values))},
        name="after",
    )(*values, *others)


def cost(flops, moved, exps=0):
    return pl.CostEstimate(flops=flops // 1000, bytes_accessed=moved // 1000, transcendentals=exps)


def attend_kernel(step, len_ref, q_ref, k_ref, v_ref, o_ref, lse_ref):
    depth = k_ref.shape[-1]
    q = q_ref[0] * (depth**-0.5)
    s = dot_t(k_ref[0], q.astype(BF))
    ids = lax.broadcasted_iota(jnp.int32, s.shape, 0)
    s = jnp.where(ids < len_ref[step], s, MASKED)
    top = jnp.max(s, axis=0, keepdims=True)
    e = jnp.exp(s - top)
    total = jnp.sum(e, axis=0, keepdims=True)
    p = (e * (1.0 / total)).astype(BF)
    o_ref[0] = dot_w(p, v_ref[0]).astype(BF)
    lse_ref[0, 0] = top + jnp.log(total)


def attend(step, qkv, lens, heads, before=(), gate=()):
    micro, rows, all_width = qkv.shape
    depth = all_width // (heads + 2)
    spec = lambda f: pl.BlockSpec((1, rows, depth), f)

    def kernel(*refs):
        attend_kernel(step, *refs)

    return pl.pallas_call(
        chained(kernel, 4, len(before) + len(gate)),
        grid_spec=pltpu.PrefetchScalarGridSpec(
            num_scalar_prefetch=1,
            grid=(heads,),
            in_specs=[
                spec(lambda h, s: (step, 0, h)),
                spec(lambda h, s: (step, 0, heads)),
                spec(lambda h, s: (step, 0, heads + 1)),
            ]
            + kept(len(before) + len(gate)),
            out_specs=[
                spec(lambda h, s: (step, 0, h)),
                pl.BlockSpec((1, 1, 1, rows), lambda h, s: (step, h, 0, 0)),
            ],
        ),
        out_shape=[
            jax.ShapeDtypeStruct((micro, rows, heads * depth), BF),
            jax.ShapeDtypeStruct((micro, heads, 1, rows), F32),
        ],
        input_output_aliases={4 + i: i for i in range(len(before))},
        compiler_params=params(48, 1),
        cost_estimate=cost(4 * heads * rows * rows * depth, 2 * rows * all_width * 2),
        name="attend",
    )(lens, qkv, qkv, qkv, *before, *gate)


def attend_back_kernel(step, len_ref, q_ref, k_ref, v_ref, do_ref, lse_ref, dq_ref, dk_ref, dv_ref):
    depth = k_ref.shape[-1]
    scale = depth**-0.5

    @pl.when(pl.program_id(0) == 0)
    def _():
        dk_ref[...] = jnp.zeros_like(dk_ref)
        dv_ref[...] = jnp.zeros_like(dv_ref)

    q = (q_ref[0] * scale).astype(BF)
    do = do_ref[0]
    s = dot_t(k_ref[0], q)
    ids = lax.broadcasted_iota(jnp.int32, s.shape, 0)
    p = jnp.where(ids < len_ref[step], jnp.exp(s - lse_ref[0, 0]), 0.0)
    dv_ref[0] += dot(p.astype(BF), do)
    dp = dot_t(v_ref[0], do)
    centre = jnp.sum(p * dp, axis=0, keepdims=True)
    ds = (p * (dp - centre)).astype(BF)
    dk_ref[0] += dot(ds, q)
    dq_ref[0] = (dot_w(ds, k_ref[0]) * scale).astype(BF)


def attend_back(step, qkv, dout, lse, lens, heads, before=(), gate=()):
    micro, rows, all_width = qkv.shape
    depth = all_width // (heads + 2)
    spec = lambda f: pl.BlockSpec((1, rows, depth), f)

    def kernel(*refs):
        attend_back_kernel(step, *refs)

    return pl.pallas_call(
        chained(kernel, 6, len(before) + len(gate)),
        grid_spec=pltpu.PrefetchScalarGridSpec(
            num_scalar_prefetch=1,
            grid=(heads,),
            in_specs=[
                spec(lambda h, s: (step, 0, h)),
                spec(lambda h, s: (step, 0, heads)),
                spec(lambda h, s: (step, 0, heads + 1)),
                spec(lambda h, s: (step, 0, h)),
                pl.BlockSpec((1, 1, 1, rows), lambda h, s: (step, h, 0, 0)),
            ]
            + kept(len(before) + len(gate)),
            out_specs=[
                spec(lambda h, s: (step, 0, h)),
                spec(lambda h, s: (step, 0, 0)),
                spec(lambda h, s: (step, 0, 0)),
            ],
        ),
        out_shape=[
            jax.ShapeDtypeStruct((micro, rows, heads * depth), BF),
            jax.ShapeDtypeStruct((micro, rows, depth), F32),
            jax.ShapeDtypeStruct((micro, rows, depth), F32),
        ],
        input_output_aliases={6 + i: i for i in range(len(before))},
        compiler_params=params(48, 1),
        cost_estimate=cost(10 * heads * rows * rows * depth, 5 * rows * all_width * 2),
        name="attend_back",
    )(lens, qkv, qkv, qkv, dout, lse, *before, *gate)


def feed_kernel(
    o_ref, x_ref, cot_ref, wm_ref, gain_ref, wg_ref, wu_ref, wd_ref,
    out_ref, dx_ref, dmixed_ref, dattn_ref, hs_ref, mid_ref, dgate_ref, dup_ref,
    h_ref, acc_ref, dh_ref,
):
    at = pl.program_id(0)
    last = pl.num_programs(0) - 1

    @pl.when(at == 0)
    def _():
        x1 = x_ref[...].astype(F32) + dot(o_ref[...], wm_ref[...])
        h = (normed(x1)[0] * gain_ref[...]).astype(BF)
        h_ref[...] = h
        hs_ref[...] = h
        acc_ref[...] = x1
        dx_ref[...] = x1
        dh_ref[...] = jnp.zeros_like(dh_ref)

    h = h_ref[...]
    dy = cot_ref[...]
    gate = dot(h, wg_ref[...])
    up = dot(h, wu_ref[...])
    dmid = dot_t(dy, wd_ref[...])
    act, slope = gelu_parts(gate)
    mid = (act * up).astype(BF)
    dgate = (dmid * up * slope).astype(BF)
    dup = (dmid * act).astype(BF)
    mid_ref[...] = mid
    dgate_ref[...] = dgate
    dup_ref[...] = dup
    acc_ref[...] += dot(mid, wd_ref[...])
    dh_ref[...] += dot_t(dgate, wg_ref[...]) + dot_t(dup, wu_ref[...])

    @pl.when(at == last)
    def _():
        out_ref[...] = acc_ref[...].astype(BF)
        normal, factor = normed(dx_ref[...])
        dh = dh_ref[...]
        dx = cot_ref[...].astype(F32) + norm_back(dh, normal, factor, gain_ref[...])
        dx_ref[...] = dx
        dmixed = dx.astype(BF)
        dmixed_ref[...] = dmixed
        dattn_ref[...] = dot_t(dmixed, wm_ref[...]).astype(BF)


def feed(step, micro, o, x, cot, wm, gain, wgu, wd, before=(), gate=()):
    total, width = x.shape
    rows = total // micro
    hq, ff = o.shape[1], wd.shape[0]
    unit = 512
    chunks = ff // unit
    once = dict(pipeline_mode=pl.Buffered(1))
    row = lambda w: pl.BlockSpec((rows, w), lambda i: (step, 0), **once)
    col = lambda f: pl.BlockSpec((rows, unit), f)
    whole = lambda a: pl.BlockSpec(a.shape, lambda i: (0, 0), **once)
    out = lambda w, t: jax.ShapeDtypeStruct((total, w), t)
    kernel = chained(feed_kernel, 8, len(before) + len(gate))
    return pl.pallas_call(
        kernel,
        grid=(chunks,),
        in_specs=[row(hq), row(width), row(width), whole(wm), whole(gain)]
        + [
            pl.BlockSpec((width, unit), lambda i: (0, i)),
            pl.BlockSpec((width, unit), lambda i: (0, chunks + i)),
            pl.BlockSpec((unit, width), lambda i: (i, 0)),
        ]
        + kept(len(before) + len(gate)),
        out_specs=[row(width), row(width), row(width), row(hq), row(width)]
        + [col(lambda i: (step, i))] * 3,
        out_shape=[
            out(width, BF), out(width, F32), out(width, BF), out(hq, BF), out(width, BF),
            out(ff, BF), out(ff, BF), out(ff, BF),
        ],
        scratch_shapes=[
            pltpu.VMEM((rows, width), BF),
            pltpu.VMEM((rows, width), F32),
            pltpu.VMEM((rows, width), F32),
        ],
        input_output_aliases={8 + i: i for i in range(len(before))},
        compiler_params=params(60, 1),
        cost_estimate=cost(rows * (12 * width * ff + 4 * width * hq), rows * ff * 8 + wgu.size * 3),
        name="feed",
    )(o, x, cot, wm, gain, wgu, wgu, wd, *before, *gate)


def weight_grad_kernel(spread, x_ref, *refs):
    if spread:
        spread_ref, *refs = refs
    *g_refs, out_ref, turned_ref = refs
    at = pl.program_id(0)

    @pl.when(at == 0)
    def _():
        if spread:
            turned_ref[...] = lax.dot_general(
                spread_ref[...],
                x_ref[...],
                (((0,), (1,)), ((), ())),
                preferred_element_type=F32,
            ).astype(BF)
        else:
            turned_ref[...] = x_ref[...].T

    each = pl.num_programs(0) // len(g_refs)
    for i, g_ref in enumerate(g_refs):

        @pl.when(at // each == i)
        def _():
            out_ref[...] = dot(turned_ref[...], g_ref[...]).astype(BF)


def weight_grad(x, grads, unit, spread=None, gate=()):
    rows, width = x.shape
    each = grads[0].shape[1] // unit
    count = each * len(grads)
    columns = count * unit
    whole = lambda a: pl.BlockSpec(a.shape, lambda at: (0, 0), pipeline_mode=pl.Buffered(1))
    extra = [] if spread is None else [spread]
    width = width if spread is None else spread.shape[1]

    def kernel(*refs):
        weight_grad_kernel(spread is not None, *refs)

    def place(i):
        return pl.BlockSpec(
            (rows, unit), lambda at: (0, jnp.clip(at - i * each, 0, each - 1))
        )

    return pl.pallas_call(
        chained(kernel, 1 + len(extra) + len(grads), len(gate)),
        grid=(count,),
        in_specs=[whole(a) for a in [x] + extra]
        + [place(i) for i in range(len(grads))]
        + kept(len(gate)),
        out_specs=pl.BlockSpec((width, unit), lambda at: (0, at)),
        out_shape=jax.ShapeDtypeStruct((width, columns), BF),
        scratch_shapes=[pltpu.VMEM((width, rows), BF)],
        compiler_params=params(48, 1),
        cost_estimate=cost(2 * rows * width * count * unit, 2 * rows * (width + count * unit)),
        name="weight_grad",
    )(x, *extra, *grads, *gate)


def stack_heads(x, heads):
    depth = x.shape[-1] // heads
    return jnp.concatenate([x[:, h * depth : (h + 1) * depth] for h in range(heads)], axis=0)


def own_scores(heads, scale, length, seg_len, qkv_ref, k_ref):
    depth = k_ref.shape[-1]
    qkv = qkv_ref[0, 0].astype(F32)
    q = (stack_heads(qkv[:, : heads * depth], heads) * scale).astype(BF)
    near_k = qkv[:, heads * depth : (heads + 1) * depth].astype(BF)
    near_v = qkv[:, (heads + 1) * depth :].astype(BF)
    far = dot_t(k_ref[0], q)
    near = dot_t(near_k, q)
    far_ok = lax.broadcasted_iota(jnp.int32, far.shape, 0) < length
    near_ok = lax.broadcasted_iota(jnp.int32, near.shape, 0) < seg_len
    return q, near_k, near_v, jnp.where(far_ok, far, MASKED), jnp.where(near_ok, near, MASKED)


def own_kernel(heads, seg_len, own_ref, len_ref, qkv_ref, k_ref, v_ref, o_ref, lse_ref):
    m, c = pl.program_id(0), pl.program_id(1)
    mine = own_ref[m * pl.num_programs(1) + c] == 1
    depth = k_ref.shape[-1]
    rows = qkv_ref.shape[2]

    @pl.when(mine)
    def _():
        q, near_k, near_v, far, near = own_scores(
            heads, depth**-0.5, len_ref[m], seg_len, qkv_ref, k_ref
        )
        top = jnp.maximum(
            jnp.max(far, axis=0, keepdims=True), jnp.max(near, axis=0, keepdims=True)
        )
        far, near = jnp.exp(far - top), jnp.exp(near - top)
        total = jnp.sum(far, axis=0, keepdims=True) + jnp.sum(near, axis=0, keepdims=True)
        part = 1.0 / total
        o = dot_w((far * part).astype(BF), v_ref[0]) + dot_w((near * part).astype(BF), near_v)
        for h in range(heads):
            o_ref[0, 0, :, h * depth : (h + 1) * depth] = o[h * rows : (h + 1) * rows].astype(BF)
        lse_ref[0, 0] = top + jnp.log(total)

    @pl.when(jnp.logical_not(mine))
    def _():
        o_ref[...] = jnp.zeros_like(o_ref)
        lse_ref[...] = jnp.zeros_like(lse_ref)


def own_attend(seg_qkv, qkv, own, lens, heads, seg_len):
    n, micro, rows, all_width = seg_qkv.shape
    depth = all_width // (heads + 2)
    prefix = qkv.shape[1]
    seg = lambda w: pl.BlockSpec((1, 1, rows, w), lambda m, c, a, b: (c, m, 0, 0))
    stat = pl.BlockSpec((1, 1, 1, heads * rows), lambda m, c, a, b: (c, m, 0, 0))

    def kernel(*refs):
        own_kernel(heads, seg_len, *refs)

    return pl.pallas_call(
        kernel,
        grid_spec=pltpu.PrefetchScalarGridSpec(
            num_scalar_prefetch=2,
            grid=(micro, n),
            in_specs=[
                seg(all_width),
                pl.BlockSpec((1, prefix, depth), lambda m, c, a, b: (m, 0, heads)),
                pl.BlockSpec((1, prefix, depth), lambda m, c, a, b: (m, 0, heads + 1)),
            ],
            out_specs=[seg(heads * depth), stat],
        ),
        out_shape=[
            jax.ShapeDtypeStruct((n, micro, rows, heads * depth), BF),
            jax.ShapeDtypeStruct((n, micro, 1, heads * rows), F32),
        ],
        compiler_params=params(32, 2),
        cost_estimate=cost(4 * 2 * micro * heads * rows * prefix * depth, 4 * seg_qkv.size),
        name="own_attend",
    )(own, lens, seg_qkv, qkv, qkv)


def own_back_kernel(
    heads, seg_len, own_ref, len_ref, qkv_ref, k_ref, v_ref, do_ref, lse_ref, dqkv_ref, dk_ref, dv_ref
):
    m, c = pl.program_id(0), pl.program_id(1)
    mine = own_ref[m * pl.num_programs(1) + c] == 1
    depth = k_ref.shape[-1]
    rows = qkv_ref.shape[2]
    scale = depth**-0.5

    @pl.when(c == 0)
    def _():
        dk_ref[...] = jnp.zeros_like(dk_ref)
        dv_ref[...] = jnp.zeros_like(dv_ref)

    @pl.when(mine)
    def _():
        q, near_k, near_v, far, near = own_scores(heads, scale, len_ref[m], seg_len, qkv_ref, k_ref)
        far, near = jnp.exp(far - lse_ref[0, 0]), jnp.exp(near - lse_ref[0, 0])
        do = stack_heads(do_ref[0, 0].astype(F32), heads).astype(BF)
        dv_ref[0] += dot(far.astype(BF), do)
        dfar, dnear = dot_t(v_ref[0], do), dot_t(near_v, do)
        centre = jnp.sum(far * dfar, axis=0, keepdims=True)
        centre = centre + jnp.sum(near * dnear, axis=0, keepdims=True)
        sfar = (far * (dfar - centre)).astype(BF)
        snear = (near * (dnear - centre)).astype(BF)
        dk_ref[0] += dot(sfar, q)
        dq = (dot_w(sfar, k_ref[0]) + dot_w(snear, near_k)) * scale
        for h in range(heads):
            dqkv_ref[0, 0, :, h * depth : (h + 1) * depth] = dq[h * rows : (h + 1) * rows].astype(BF)
        dqkv_ref[0, 0, :, heads * depth : (heads + 1) * depth] = dot(snear, q).astype(BF)
        dqkv_ref[0, 0, :, (heads + 1) * depth :] = dot(near.astype(BF), do).astype(BF)

    @pl.when(jnp.logical_not(mine))
    def _():
        dqkv_ref[...] = jnp.zeros_like(dqkv_ref)


def own_back(seg_qkv, qkv, dout, lse, own, lens, heads, seg_len):
    n, micro, rows, all_width = seg_qkv.shape
    depth = all_width // (heads + 2)
    prefix = qkv.shape[1]
    seg = lambda w: pl.BlockSpec((1, 1, rows, w), lambda m, c, a, b: (c, m, 0, 0))
    item = lambda i: pl.BlockSpec((1, prefix, depth), lambda m, c, a, b: (m, 0, i))

    def kernel(*refs):
        own_back_kernel(heads, seg_len, *refs)

    return pl.pallas_call(
        kernel,
        grid_spec=pltpu.PrefetchScalarGridSpec(
            num_scalar_prefetch=2,
            grid=(micro, n),
            in_specs=[
                seg(all_width),
                item(heads),
                item(heads + 1),
                seg(heads * depth),
                pl.BlockSpec((1, 1, 1, heads * rows), lambda m, c, a, b: (c, m, 0, 0)),
            ],
            out_specs=[seg(all_width), item(0), item(0)],
        ),
        out_shape=[
            jax.ShapeDtypeStruct((n, micro, rows, all_width), BF),
            jax.ShapeDtypeStruct((micro, prefix, depth), F32),
            jax.ShapeDtypeStruct((micro, prefix, depth), F32),
        ],
        compiler_params=params(32, 2),
        cost_estimate=cost(10 * 2 * micro * heads * rows * prefix * depth, 8 * seg_qkv.size),
        name="own_back",
    )(own, lens, seg_qkv, qkv, qkv, dout, lse)


def per_device(
    prefix_rows,
    action_rows,
    segment_item,
    segment_time,
    item_weight,
    prefix_len,
    vlm_prenorm,
    vlm_query,
    vlm_key,
    vlm_value,
    vlm_mixer,
    vlm_midnorm,
    vlm_gate,
    vlm_expand,
    vlm_down,
    act_prenorm,
    act_query,
    act_key,
    act_value,
    act_mixer,
    act_midnorm,
    act_gate,
    act_expand,
    act_down,
    time_scales,
    cot_prefix,
    cot_action,
):
    micro, items, prefix, width = prefix_rows.shape
    seg_len, wide = action_rows.shape[2:]
    groups, n = lax.axis_size("dp"), lax.axis_size("noise")
    depth, hq = vlm_key.shape[1], vlm_query.shape[1]
    heads = hq // depth
    width_qkv = hq + 2 * depth
    ff, ffa = vlm_gate.shape[1], act_gate.shape[1]
    levels = time_scales.shape[1]
    rows_p, rows_a = vlm_query.shape[0], act_query.shape[0]
    here = lax.axis_index("noise")
    every, line = Line(ALL), Line("noise")
    total = every.count
    dp = Line("dp")
    slot = -(-(seg_len + 1) // 8) * 8
    block = micro * slot

    lanes = lambda x, w: jnp.pad(x, ((0, 0), (0, w - x.shape[1])))
    gap = -(-rows_p // 8) * 8
    taller = lambda x: jnp.pad(x, ((0, gap - rows_p), (0, 0)))
    rows_m = vlm_mixer.shape[0]
    unit = act_down.shape[0]
    part = groups * unit

    item, time = segment_item[:, 0], segment_time[:, 0]
    spare = jnp.zeros((micro, slot - seg_len, wide), BF)
    tags = spare.at[:, 0, 0].set(item.astype(BF)).at[:, 0, 1].set(time.astype(BF))
    action_in = jnp.concatenate([action_rows[:, 0], tags], axis=1)
    hot = item[:, None] == jnp.arange(prefix_len.shape[1])[None, :]
    weight = (jnp.sum(jnp.where(hot, item_weight, 0), axis=1) + 1).astype(F32) / 8.0
    grad_action = cot_action[:, 0].astype(F32) * weight[:, None, None]
    grad_action = jnp.pad(grad_action, ((0, 0), (0, slot - seg_len), (0, 0)))

    pre_pack = jnp.concatenate(
        [
            vlm_query,
            vlm_key,
            vlm_value,
            lanes(jnp.stack([vlm_prenorm, vlm_midnorm], axis=1), 128),
        ],
        axis=1,
    )
    act_small = [act_prenorm[:, None], act_midnorm[:, None], time_scales.reshape(rows_a, -1)]
    act_pack = [act_query, act_key, act_value, lanes(jnp.concatenate(act_small, axis=1), 128)]
    act_pack = jnp.concatenate(act_pack, axis=1)
    fold = jnp.concatenate([vlm_mixer, vlm_down], axis=0)
    second = [taller(vlm_gate), taller(vlm_expand), tiles(fold, gap), tiles(act_mixer, gap)]
    cut = 2 * ff + second[2].shape[1]
    second = lax.all_gather(jnp.concatenate(second, axis=1), ALL, axis=0)

    def beside(near):
        cols = jnp.stack([act_gate, act_expand]).reshape(2, rows_a, groups, n, unit)
        cols = cols.transpose(3, 0, 1, 2, 4).reshape(n, 2, rows_a, part)
        (cols,) = after([cols], near)
        return lax.all_to_all(cols, "noise", 0, 0, tiled=True)

    first = jnp.concatenate([act_pack, taller(pre_pack)], axis=0)
    first, seg_all, cols = fetch(first, action_in, dp, line, beside)
    cols = cols.transpose(0, 2, 1, 3).reshape(n * rows_a, 2 * part)
    hidden_w = jnp.concatenate([cols, act_down.reshape(-1, 2 * part)], axis=0)
    hidden_w = lax.all_gather(hidden_w, "dp", axis=0)
    dy_own = grad_action.astype(BF).reshape(block, wide)
    act_a = first[:, :rows_a].reshape(total * rows_a, -1)
    pre_a = first[:, rows_a:].reshape(total * gap, -1)

    places = jnp.arange(total * gap)
    spread = (places // gap * rows_p + places % gap)[None, :] == jnp.arange(width)[:, None]
    spread = (spread & (places % gap < rows_p)[None, :]).astype(BF)
    pre_a = dot(spread, pre_a).astype(BF)
    pre_qkv = pre_a[:, :width_qkv]
    pre_gain = pre_a[:, width_qkv].astype(F32)
    pre_midgain = pre_a[:, width_qkv + 1].astype(F32)
    suf_qkv = act_a[:, :width_qkv]
    small = act_a[:, width_qkv:].astype(F32)
    suf_gain, suf_midgain = small[:, 0], small[:, 1]
    table = small[:, 2 : 2 + time_scales.size // rows_a].reshape(2 * wide, levels)

    times = seg_all[:, :, seg_len, 1].astype(jnp.int32)
    own = (seg_all[:, :, seg_len, 0].astype(jnp.int32) == here).astype(jnp.int32)
    own = own.T.reshape(-1)
    is_row = (jnp.arange(slot) < seg_len)[:, None]
    hots = (times[..., None] == jnp.arange(levels)).astype(F32)
    mods = jnp.einsum("nmt,jt->nmj", hots, table, precision=HIGH)
    mod1_all = mods[:, :, None, :wide]
    mod2 = mods[0, :, None, wide:]
    an1, as1 = normed(jnp.where(is_row, seg_all, 0).astype(F32))
    ah1 = flatten((an1 * suf_gain * mod1_all).astype(BF))
    seg_qkv = dot(ah1, suf_qkv).astype(BF).reshape(n, micro, slot, width_qkv)

    x = prefix_rows[:, 0]
    n1, s1 = normed(x.astype(F32))
    h1 = flatten((n1 * pre_gain).astype(BF))
    qkv = dot(h1, pre_qkv).astype(BF).reshape(micro, prefix, width_qkv)
    lens = lax.dynamic_slice_in_dim(prefix_len, here, 1, axis=1)[:, 0]

    oa, lse_a = own_attend(seg_qkv, qkv, own, lens, heads, seg_len)

    oa = line.home(oa.reshape(n, block, hq))
    (dy_own,) = after([dy_own], oa)
    dy_all = line.around(dy_own).reshape(-1, wide)
    gu_w = hidden_w[:, : n * rows_a].reshape(-1, 2 * part)
    down_w = hidden_w[:, n * rows_a :].reshape(part, wide)
    outs = attend(0, qkv, lens, heads, (), (seg_qkv,))
    outs = attend(1, qkv, lens, heads, outs, (oa,))
    o, lse = outs
    oa = line.home_end(oa, (o,)).astype(BF)
    suf_mixer = tiles(second[..., cut:], gap, act_mixer.shape)
    a1 = jnp.where(is_row, action_in, 0).astype(F32) + dot(oa, suf_mixer).reshape(micro, slot, wide)
    an2, as2 = normed(a1)
    ah2 = (an2 * suf_midgain * mod2).astype(BF).reshape(block, wide)

    pre_gu = dot(spread, second[..., : 2 * ff].reshape(total * gap, -1)).astype(BF)
    fold = tiles(second[..., 2 * ff : cut], gap, fold.shape).reshape(total, -1, width)
    pre_mixer = fold[:, :rows_m].reshape(hq, width)
    pre_down = fold[:, rows_m:].reshape(ff, width)
    h_all = line.around(ah2, (pre_gu, pre_mixer, pre_down)).reshape(n * block, wide)
    gu = dot(h_all, gu_w)
    gate_a, up_a = gu[:, :part], gu[:, part:]
    act_g, slope_g = gelu_parts(gate_a)
    mid_a = (act_g * up_a).astype(BF)
    dmid_a = dot_t(dy_all, down_w)
    dgu = jnp.concatenate(
        [(dmid_a * up_a * slope_g).astype(BF), (dmid_a * act_g).astype(BF)], axis=1
    )
    grad_late = line.home(dot_t(dgu, gu_w).astype(BF).reshape(n, block, wide))
    out_a = turned(dot(mid_a, down_w).astype(BF).reshape(n, block, wide), here)
    out_a = lax.psum_scatter(out_a, "noise", scatter_dimension=0)
    dff = jnp.concatenate(
        [
            dot_w(h_all, dgu).astype(BF).reshape(groups, n * rows_a, 2 * part),
            dot_w(mid_a, dy_all).astype(BF).reshape(groups, -1, 2 * part),
        ],
        axis=1,
    )
    dff = dff.reshape(-1, 2 * part)
    dff = lax.psum_scatter(dff, "dp", scatter_dimension=0, tiled=True)

    cot = cot_prefix.reshape(micro * prefix, width)

    def feed_half(step, outs, gate):
        return feed(
            step, micro, o.reshape(-1, hq), x.reshape(-1, width), cot,
            pre_mixer, pre_midgain[None], pre_gu, pre_down, outs, gate,
        )

    outs = feed_half(0, (), (grad_late,))
    grad_late = line.home_end(grad_late, (outs[0],)).reshape(micro, slot, wide)
    late_back = grad_late * an2
    dmod2 = jnp.sum(late_back * suf_midgain, axis=1)
    da1 = grad_action + norm_back(grad_late, an2, as2, suf_midgain * mod2)
    dmixed_a = da1.astype(BF).reshape(block, wide)
    dattn_a = dot_t(dmixed_a, suf_mixer).astype(BF)
    outs = feed_half(1, outs, (dattn_a,))
    prefix_out, dx1, dmixed, dattn, h2, mid, dgate, dup = outs
    dattn_all = line.around(dattn_a, (dx1,)).reshape(n, micro, slot, hq)

    big_w = weight_grad(h2, [dgate, dup], 512, spread)
    big_sum = Sum(big_w.reshape(total, gap, -1), dp, line)
    big_way = joint(big_sum.cores())

    (dattn_all,) = after([dattn_all], big_w)
    dseg, far_dk, far_dv = own_back(seg_qkv, qkv, dattn_all, lse_a, own, lens, heads, seg_len)
    dseg = dseg.reshape(n * block, width_qkv)
    dah1 = dot_t(dseg, suf_qkv).reshape(n, micro, slot, wide)
    dmod1 = jnp.sum(dah1 * an1 * suf_gain, axis=2)
    back = norm_back(dah1, an1, as1, suf_gain * mod1_all).astype(BF).reshape(n, block, wide)
    dtable = jnp.concatenate(
        [
            jnp.einsum("nmj,nmt->jt", dmod1, hots, precision=HIGH),
            jnp.einsum("mj,mt->jt", dmod2, hots[0], precision=HIGH),
        ],
        axis=0,
    )
    table_cols = dtable.size // wide
    dtable = lanes(dtable.reshape(wide, table_cols), 128).astype(BF)
    act_w = jnp.concatenate([dot_w(ah1, dseg).astype(BF), dtable], axis=1)
    act_sum = Sum(act_w.reshape(total, rows_a, -1), dp, line)
    big_sum.take(big_way)

    early = (big_sum.x, act_w)
    dmd_w = jnp.concatenate(
        [
            weight_grad(o.reshape(-1, hq), [dmixed], width, gate=early).reshape(
                total, rows_m, width
            ),
            weight_grad(mid, [cot], width, gate=early).reshape(total, -1, width),
        ],
        axis=1,
    )
    grads = [dmd_w, dot_w(oa, dmixed_a).astype(BF).reshape(total, rows_a, -1)]
    grads = [jax.vmap(lambda g: tiles(g, gap))(g) for g in grads]
    cut = grads[0].shape[-1]
    grads = jnp.concatenate(grads, axis=-1)
    grads_sum = lax.psum_scatter(grads, ALL, scatter_dimension=0)
    dmd_w = tiles(grads_sum[:, :cut], gap, dmd_w.shape[1:])
    dam_w = tiles(grads_sum[:, cut:], gap, (rows_a, wide))

    dattn = dattn.reshape(micro, prefix, hq)
    outs = attend_back(0, qkv, dattn, lse, lens, heads, (), (grads,))
    *big_way, act_way = joint(big_sum.groups() + act_sum.cores(), outs[0])
    big_sum.take(big_way)
    act_sum.take([act_way])
    outs = attend_back(1, qkv, dattn, lse, lens, heads, outs, (big_sum.x, act_sum.x))
    dq, dk, dv = outs
    big_way, *act_way = joint(big_sum.along() + act_sum.groups(), dq)
    big_sum.take([big_way])
    act_sum.take(act_way)
    dkv = jnp.concatenate([(dk + far_dk).astype(BF), (dv + far_dv).astype(BF)], axis=-1)
    dqkv = jnp.concatenate([dq, dkv], axis=-1).reshape(-1, width_qkv)
    pre_w = weight_grad(h1, [dqkv], 512, spread, (big_sum.x, act_sum.x))
    back = back.reshape((n // 2, 2) + back.shape[1:])
    jobs = [big_sum.along() if big_sum.bits else [], act_sum.along(), [(line, back[:, 1], 1)]]
    *ways, back_way = joint(sum(jobs, []), pre_w)
    for way, each in zip(ways, [s for s, j in zip((big_sum, act_sum), jobs) if j]):
        each.take([way])
    back = back[:, 0] + back_way
    pre_sum = Sum(pre_w.reshape(total, gap, -1), dp, line)
    jobs = act_sum.along() if act_sum.bits else []
    *ways, pre_way = joint(jobs + pre_sum.cores(), back)
    for way in ways:
        act_sum.take([way])
    pre_sum.take([pre_way])
    pre_sum.take(joint(pre_sum.groups()))
    (dqkv, back) = after([dqkv, back], pre_w)

    (dff,) = after([dff], pre_w)
    ddown_a = dff[n * rows_a :].reshape(unit, wide)
    dgu_a = dff[: n * rows_a].reshape(n, rows_a, 2 * part)
    dgu_a = lax.all_to_all(dgu_a, "noise", 0, 0, tiled=True)
    dgu_a = dgu_a.reshape(n, rows_a, 2, groups, unit).transpose(2, 1, 3, 0, 4)
    dgu_a = dgu_a.reshape(2, rows_a, ffa).astype(F32)
    back = line.home_end(back).reshape(micro, slot, wide)
    action_out = (a1 + out_a.reshape(micro, slot, wide))[:, :seg_len].astype(BF)
    action_grad = (da1 + back)[:, :seg_len]
    dh1 = dot_t(dqkv, pre_qkv).reshape(micro, prefix, width)
    prefix_grad = dx1.reshape(micro, prefix, width) + norm_back(dh1, n1, s1, pre_gain)

    big_g = big_sum.result()[:rows_p]
    act_g = act_sum.result()
    pre_g = pre_sum.result()[:rows_p]

    def gain_grad(pairs, gain):
        sums = sum(jnp.sum(w.astype(F32) * dw, axis=1) for w, dw in pairs)
        return sums / gain.astype(F32)

    pre_pairs = [
        (vlm_query, pre_g[:, :hq]),
        (vlm_key, pre_g[:, hq : hq + depth]),
        (vlm_value, pre_g[:, hq + depth :]),
    ]
    mid_pairs = [(vlm_gate, big_g[:, :ff]), (vlm_expand, big_g[:, ff:])]
    act_pairs = [
        (act_query, act_g[:, :hq]),
        (act_key, act_g[:, hq : hq + depth]),
        (act_value, act_g[:, hq + depth : width_qkv]),
    ]
    late_pairs = [(act_gate, dgu_a[0]), (act_expand, dgu_a[1])]
    return (
        prefix_out.reshape(prefix_rows.shape),
        action_out[:, None],
        prefix_grad[:, None],
        action_grad[:, None],
        gain_grad(pre_pairs, vlm_prenorm),
        pre_g[:, :hq],
        pre_g[:, hq : hq + depth],
        pre_g[:, hq + depth :],
        dmd_w[:rows_m].astype(F32),
        gain_grad(mid_pairs, vlm_midnorm),
        big_g[:, :ff],
        big_g[:, ff:],
        dmd_w[rows_m:].astype(F32),
        gain_grad(act_pairs, act_prenorm),
        act_g[:, :hq],
        act_g[:, hq : hq + depth],
        act_g[:, hq + depth : width_qkv],
        dam_w.astype(F32),
        gain_grad(late_pairs, act_midnorm),
        dgu_a[0],
        dgu_a[1],
        ddown_a.astype(F32),
        act_g[:, width_qkv : width_qkv + table_cols].reshape(-1, levels),
    )


def solution(mesh):
    return jax.shard_map(
        per_device,
        mesh=mesh,
        in_specs=(
            P(None, ("dp", "noise"), None, None),
            P(None, ("dp", "noise"), None, None),
            P(None, ("dp", "noise")),
            P(None, ("dp", "noise")),
            P(None, "dp"),
            P(None, "dp"),
            P(("dp", "noise")),
            P(("dp", "noise"), None),
            P(("dp", "noise"), None),
            P(("dp", "noise"), None),
            P(("dp", "noise"), None),
            P(("dp", "noise")),
            P(("dp", "noise"), None),
            P(("dp", "noise"), None),
            P(("dp", "noise"), None),
            P(("dp", "noise")),
            P(("dp", "noise"), None),
            P(("dp", "noise"), None),
            P(("dp", "noise"), None),
            P(("dp", "noise"), None),
            P(("dp", "noise")),
            P(("dp", "noise"), None),
            P(("dp", "noise"), None),
            P(("dp", "noise"), None),
            P(("dp", "noise"), None),
            P(None, ("dp", "noise"), None, None),
            P(None, ("dp", "noise"), None, None),
        ),
        out_specs=(
            P(None, ("dp", "noise"), None, None),
            P(None, ("dp", "noise"), None, None),
            P(None, ("dp", "noise"), None, None),
            P(None, ("dp", "noise"), None, None),
            P(("dp", "noise")),
            P(("dp", "noise"), None),
            P(("dp", "noise"), None),
            P(("dp", "noise"), None),
            P(("dp", "noise"), None),
            P(("dp", "noise")),
            P(("dp", "noise"), None),
            P(("dp", "noise"), None),
            P(("dp", "noise"), None),
            P(("dp", "noise")),
            P(("dp", "noise"), None),
            P(("dp", "noise"), None),
            P(("dp", "noise"), None),
            P(("dp", "noise"), None),
            P(("dp", "noise")),
            P(("dp", "noise"), None),
            P(("dp", "noise"), None),
            P(("dp", "noise"), None),
            P(("dp", "noise"), None),
        ),
        check_vma=False,
    )
```
